512 devices in a mesh: expert: 8 (over z_hi, core), tensor: 64 (over y, z_lo, x).
Axes of the slice: x: 4, y: 4, z: 16 (z_hi: 4, z_lo: 4; z = z_hi * 4 + z_lo), core: 2. Of those that a mesh axis runs over, the one named last changes fastest.
Arguments:
- tokens: bfloat16 [1024, 4096], P('tensor'), may hold values from -6 to 6
- cotangent: bfloat16 [1024, 4096], P('tensor'), may hold values from -6 to 6
- expert_id: int32 [1024], P('tensor'), may hold values from 0 to 7, as said below
- gate_weight: bfloat16 [8, 4096, 8192], P('expert', None, 'tensor'), may hold values from -0.09375 to 0.09375
- up_weight: bfloat16 [8, 4096, 8192], P('expert', None, 'tensor'), may hold values from -0.09375 to 0.09375
- down_weight: bfloat16 [8, 8192, 4096], P('expert', 'tensor'), may hold values from -0.0625 to 0.0625
Outputs:
- layer_out: bfloat16 [1024, 4096], P('tensor')
- grad_in: bfloat16 [1024, 4096], P('tensor')
The draws below stay inside these ranges and needn't reach their ends.
Inputs may be any that keep to these rules, and one draw needn't show every extreme that they name: `expert_id`: the 16 rows of each owner name every expert at most 4 times; every expert is named 4 times by some owner.
All inputs are finite; a program needn't handle non-finite values.
Results may differ from the reference program's by a relative error of at most 0.005.
Values may be sent and summed in bfloat16 or wider, within the bound.
No kernel may reach another device: no remote copies, remote signals or barrier semaphores. Data moves between devices by JAX's collectives and lax.ppermute only.
A program may use at most 64 MiB of HBM per device.

```python
import jax
import jax.numpy as jnp
from jax import lax

D = 4096
FF = 8192
SEND = 4
EXPERTS = 8
ROW_DEV = 16
ROWS = 1024
CAP = 256


def draw_expert_id(key, part):
    key = jax.random.fold_in(key, 11)
    blocks = ROWS // ROW_DEV
    cells = EXPERTS * SEND
    second, third = jax.random.split(key, 2)
    block_ids = jnp.arange(blocks, dtype=jnp.int32)
    full = jnp.where(block_ids < EXPERTS, block_ids, -5)
    ranks = jax.vmap(lambda k: jax.random.permutation(k, cells))(jax.random.split(second, blocks)).astype(jnp.int32)
    cell_ids = jnp.arange(cells, dtype=jnp.int32)
    priority = jnp.where(cell_ids[None, :] // SEND == full[:, None], -1, ranks)
    chosen = jnp.argsort(priority, axis=1, stable=True)[:, :ROW_DEV].astype(jnp.int32)
    mixed = jax.vmap(lambda k, o: jax.random.permutation(k, o))(jax.random.split(third, blocks), chosen)
    return (mixed // SEND).reshape(-1).astype(jnp.int32)


def steps_of(key, dims, cuts, low, largest):
    def one(dim, blocks):
        heights = jax.random.uniform(jax.random.fold_in(jax.random.fold_in(key, 6), dim), (blocks,), jnp.float32, low / len(cuts), largest / len(cuts))
        return jnp.repeat(jnp.exp(heights), dims[dim] // blocks).reshape((-1,) + (1,) * (len(dims) - dim - 1))

    factor_of = one(*cuts[0])
    for cut in cuts[1:]:
        factor_of = factor_of * one(*cut)
    return factor_of


def normal_values(key, dims, deviation, limit, cuts=(), held_as=jnp.bfloat16):
    values = deviation * jax.random.normal(key, dims, jnp.float32)
    if cuts:
        values = values * steps_of(key, dims, cuts, -0.22, 0.18)
    return jnp.clip(values, -limit, limit).astype(held_as)


def setup_inputs(seed: int = 0) -> dict:
    key_list = jax.random.split(jax.random.key(seed), 7)
    tokens = normal_values(key_list[0], (ROWS, D), 1.0, 6.0, ((0, 64),))
    cotangent = normal_values(key_list[1], (ROWS, D), 1.0, 6.0, ((0, 64),))
    expert_id = draw_expert_id(jax.random.fold_in(key_list[6], 71), 0)
    gate_weight = normal_values(key_list[3], (EXPERTS, D, FF), D ** -0.5, 0.09375, ((0, 8), (2, 64)))
    up_weight = normal_values(key_list[4], (EXPERTS, D, FF), D ** -0.5, 0.09375, ((0, 8), (2, 64)))
    down_weight = normal_values(key_list[5], (EXPERTS, FF, D), FF ** -0.5, 0.0625, ((0, 8), (1, 64)))
    return {"tokens": tokens, "cotangent": cotangent, "expert_id": expert_id, "gate_weight": gate_weight, "up_weight": up_weight, "down_weight": down_weight}


def contract_last(left, right):
    return lax.dot_general(left, right, (((1,), (1,)), ((), ())), preferred_element_type=jnp.float32)


def contract_first(left, right):
    return lax.dot_general(left, right, (((0,), (0,)), ((), ())), preferred_element_type=jnp.float32)


def slots_of(owner_ids):
    count = owner_ids.shape[-1]
    earlier = jnp.arange(count, dtype=jnp.int32)[:, None] > jnp.arange(count, dtype=jnp.int32)[None, :]
    same = owner_ids[..., :, None] == owner_ids[..., None, :]
    return jnp.sum((same & earlier).astype(jnp.int32), axis=-1).astype(jnp.int32)


def reference(tokens, cotangent, expert_id, gate_weight, up_weight, down_weight):
    slot = slots_of(expert_id.reshape(ROWS // ROW_DEV, ROW_DEV)).reshape(ROWS)
    owner = jnp.arange(ROWS, dtype=jnp.int32) // ROW_DEV
    target = owner * SEND + slot
    cells = jnp.arange(CAP, dtype=jnp.int32)

    def one_expert(carry, index):
        table = ((expert_id[None, :] == index) & (target[None, :] == cells[:, None])).astype(jnp.bfloat16)
        expert_rows = jnp.dot(table, tokens, preferred_element_type=jnp.float32).astype(jnp.bfloat16)
        grad_rows = jnp.dot(table, cotangent, preferred_element_type=jnp.float32).astype(jnp.bfloat16)
        w_gate = gate_weight[index]
        w_up = up_weight[index]
        w_down = down_weight[index]
        gate_pre = jnp.dot(expert_rows, w_gate, preferred_element_type=jnp.float32)
        upper = jnp.dot(expert_rows, w_up, preferred_element_type=jnp.float32)
        sigmoid_gate = jax.nn.sigmoid(gate_pre)
        hidden = (gate_pre * sigmoid_gate * upper).astype(jnp.bfloat16)
        out_rows = jnp.dot(hidden, w_down, preferred_element_type=jnp.float32).astype(jnp.bfloat16)
        d_hidden = contract_last(grad_rows, w_down)
        d_gate = (d_hidden * upper * sigmoid_gate * (1.0 + gate_pre * (1.0 - sigmoid_gate))).astype(jnp.bfloat16)
        d_up = (d_hidden * gate_pre * sigmoid_gate).astype(jnp.bfloat16)
        din_rows = (contract_last(d_gate, w_gate) + contract_last(d_up, w_up)).astype(jnp.bfloat16)
        forward_total = carry[0] + contract_first(table, out_rows)
        grad_total = carry[1] + contract_first(table, din_rows)
        return (forward_total, grad_total), None

    zeros = jnp.zeros((ROWS, D), jnp.float32)
    totals, unused = lax.scan(one_expert, (zeros, zeros), jnp.arange(EXPERTS, dtype=jnp.int32))
    return totals[0].astype(jnp.bfloat16), totals[1].astype(jnp.bfloat16)
```

```python
import functools

import jax
import jax.numpy as jnp
from jax import lax
from jax.experimental import pallas as pl
from jax.experimental.pallas import tpu as pltpu
from jax.sharding import Mesh, PartitionSpec as P

SEND = 4
AXES = ("zh", "c", "y", "zl", "x")
SIZES = (4, 2, 4, 4, 4)


def device(zh, c, y, zl, x):
    return (((zh * 2 + c) * 4 + y) * 4 + zl) * 4 + x


def mixed_groups(first):
    groups = []
    for zh in range(4):
        for c in range(2):
            for zl in range(4):
                for still in range(4):
                    if (c == 0) == (first == "x"):
                        groups.append([device(zh, c, still, zl, k) for k in range(4)])
                    else:
                        groups.append([device(zh, c, k, zl, still) for k in range(4)])
    return groups


def spread(block, axis, groups=None):
    copies = jnp.broadcast_to(block[None], (4,) + block.shape)
    return lax.all_to_all(copies, axis, 0, 0, axis_index_groups=groups, tiled=True)


def fold(blocks, axis, groups=None):
    got = lax.all_to_all(blocks, axis, 0, 0, axis_index_groups=groups, tiled=True)
    return jnp.sum(got.astype(jnp.float32), axis=0).astype(jnp.bfloat16)


def expert_kernel(steps, rows_ref, wg_ref, wu_ref, wd_ref, out_ref, gu, dh, hid, dgu):
    step = pl.program_id(0)
    half = gu.shape[1] // 2
    rows = gu.shape[0]

    @pl.when(step == 0)
    def _():
        gu[...] = jnp.zeros_like(gu)
        dh[...] = jnp.zeros_like(dh)

    @pl.when(step < steps)
    def _():
        tok = rows_ref[:, 0].reshape(rows, -1)
        cot = rows_ref[:, 1].reshape(rows, -1)
        both = jnp.concatenate([wg_ref[...], wu_ref[...]], axis=1)
        gu[...] += jnp.dot(tok, both, preferred_element_type=jnp.float32)
        dh[...] += lax.dot_general(
            cot, wd_ref[...], (((1,), (1,)), ((), ())), preferred_element_type=jnp.float32
        )

    @pl.when(step == steps - 1)
    def _():
        gate, upper, dhid = gu[:, :half], gu[:, half:], dh[...]
        s = jax.nn.sigmoid(gate)
        hid[...] = (gate * s * upper).astype(jnp.bfloat16)
        dgu[:, :half] = (dhid * upper * s * (1.0 + gate * (1.0 - s))).astype(jnp.bfloat16)
        dgu[:, half:] = (dhid * gate * s).astype(jnp.bfloat16)

    @pl.when(step >= steps)
    def _():
        both = jnp.concatenate([wg_ref[...], wu_ref[...]], axis=1)
        out = jnp.dot(hid[...], wd_ref[...], preferred_element_type=jnp.float32)
        out_ref[:, 0] = out.astype(jnp.bfloat16).reshape(out_ref.shape[0], 16, -1)
        din = lax.dot_general(
            dgu[...], both, (((1,), (1,)), ((), ())), preferred_element_type=jnp.float32
        )
        out_ref[:, 1] = din.astype(jnp.bfloat16).reshape(out_ref.shape[0], 16, -1)


def expert_call(rows, wg, wu, wd):
    steps = 4
    blocks, _, deep, width = rows.shape
    chunk = width // steps
    count = blocks * deep
    hidden = wg.shape[1]
    return pl.pallas_call(
        functools.partial(expert_kernel, steps),
        grid=(2 * steps,),
        in_specs=[
            pl.BlockSpec((blocks, 2, deep, chunk), lambda i: (0, 0, 0, jnp.minimum(i, steps - 1))),
            pl.BlockSpec((chunk, hidden), lambda i: (lax.rem(i, steps), 0)),
            pl.BlockSpec((chunk, hidden), lambda i: (lax.rem(i, steps), 0)),
            pl.BlockSpec((hidden, chunk), lambda i: (0, lax.rem(i, steps))),
        ],
        out_specs=pl.BlockSpec(
            (blocks, 2, deep, chunk), lambda i: (0, 0, 0, jnp.maximum(i - steps, 0))
        ),
        out_shape=jax.ShapeDtypeStruct(rows.shape, jnp.bfloat16),
        scratch_shapes=[
            pltpu.VMEM((count, 2 * hidden), jnp.float32),
            pltpu.VMEM((count, hidden), jnp.float32),
            pltpu.VMEM((count, hidden), jnp.bfloat16),
            pltpu.VMEM((count, 2 * hidden), jnp.bfloat16),
        ],
        compiler_params=pltpu.CompilerParams(vmem_limit_bytes=32 * 1024 * 1024),
        cost_estimate=pl.CostEstimate(
            flops=12 * count * width * hidden, bytes_accessed=14 << 20, transcendentals=count * hidden
        ),
    )(rows, wg, wu, wd)


def shards(tokens, cotangent, expert_id, gate_weight, up_weight, down_weight):
    core = lax.axis_index("c")
    my_expert = lax.axis_index("zh") * 2 + core
    count, width = tokens.shape
    earlier = (
        jnp.arange(count, dtype=jnp.int32)[:, None] > jnp.arange(count, dtype=jnp.int32)[None, :]
    )
    slot = jnp.sum(((expert_id[:, None] == expert_id[None, :]) & earlier).astype(jnp.int32), axis=1)
    positions = jnp.arange(SEND, dtype=jnp.int32)
    selector = ((expert_id[None, :] == my_expert) & (slot[None, :] == positions[:, None])).astype(
        jnp.bfloat16
    )
    own_rows = jnp.dot(selector, tokens, preferred_element_type=jnp.float32)
    own_grads = jnp.dot(selector, cotangent, preferred_element_type=jnp.float32)
    own = jnp.stack([own_rows, own_grads]).astype(jnp.bfloat16)

    first, second = mixed_groups("x"), mixed_groups("y")
    part = spread(own, "zl")
    part = jnp.swapaxes(part, 0, 1).reshape(2, 16, width)
    part = spread(part, AXES, first)
    part = spread(part, AXES, second)
    done = expert_call(
        part.reshape(16, 2, 16, width), gate_weight[0], up_weight[0], down_weight[0]
    )
    part = fold(done.reshape(4, 4, 2, 16, width), AXES, second)
    part = fold(part, AXES, first)
    part = jnp.swapaxes(part.reshape(2, 4, SEND, width), 0, 1)
    mine = fold(part, "zl")

    mine = spread(mine, "zh")
    other = lax.ppermute(mine, "c", [(0, 1), (1, 0)])

    def cells(c):
        expert = (jnp.arange(4, dtype=jnp.int32) * 2 + c)[:, None, None]
        return ((expert_id[None, None, :] == expert) & (slot[None, None, :] == positions[:, None])).astype(
            jnp.bfloat16
        ).reshape(16, count)

    def back(index):
        both = jnp.concatenate([mine[:, index].reshape(16, width), other[:, index].reshape(16, width)])
        table = jnp.concatenate([cells(core), cells(1 - core)])
        return lax.dot_general(
            table, both, (((0,), (0,)), ((), ())), preferred_element_type=jnp.float32
        ).astype(jnp.bfloat16)

    return (back(0), back(1))


def solution(mesh):
    fine = Mesh(mesh.devices.reshape(SIZES), AXES)
    tensor, expert = ("y", "zl", "x"), ("zh", "c")
    placed = (
        P(tensor, None),
        P(tensor, None),
        P(tensor),
        P(expert, None, tensor),
        P(expert, None, tensor),
        P(expert, tensor, None),
    )
    return jax.shard_map(
        shards,
        mesh=fine,
        in_specs=placed,
        out_specs=(P(tensor, None), P(tensor, None)),
        check_vma=False,
    )
```

```python
import functools

import jax
import jax.numpy as jnp
from jax import lax
from jax.experimental import pallas as pl
from jax.experimental.pallas import tpu as pltpu
from jax.sharding import Mesh, PartitionSpec as P

SEND = 4
AXES = ("zh", "c", "y", "zl", "x")
SIZES = (4, 2, 4, 4, 4)


def device(zh, c, y, zl, x):
    return (((zh * 2 + c) * 4 + y) * 4 + zl) * 4 + x


def mixed_groups(first):
    groups = []
    for zh in range(4):
        for c in range(2):
            for zl in range(4):
                for still in range(4):
                    if (c == 0) == (first == "x"):
                        groups.append([device(zh, c, still, zl, k) for k in range(4)])
                    else:
                        groups.append([device(zh, c, k, zl, still) for k in range(4)])
    return groups


def spread(block, axis, groups=None):
    copies = jnp.broadcast_to(block[None], (4,) + block.shape)
    return lax.all_to_all(copies, axis, 0, 0, axis_index_groups=groups, tiled=True)


def fold(blocks, axis, groups=None):
    got = lax.all_to_all(blocks, axis, 0, 0, axis_index_groups=groups, tiled=True)
    return jnp.sum(got.astype(jnp.float32), axis=0).astype(jnp.bfloat16)


def along(step):
    pairs = []
    for zh in range(4):
        for zl in range(4):
            for y in range(4):
                for x in range(4):
                    pairs.append((device(zh, 0, y, zl, x), device(zh, 0, (y + step) % 4, zl, x)))
                    pairs.append((device(zh, 1, y, zl, x), device(zh, 1, y, zl, (x + step) % 4)))
    return pairs


def right(block):
    return lax.ppermute(block, AXES, along(1))


def left(block):
    return lax.ppermute(block, AXES, along(3))


def block_kernel(number, *refs):
    ins, (wg_ref, wu_ref, wd_ref), outs = refs[:number], refs[number : number + 3], refs[number + 3 :]
    width, hidden = wg_ref.shape
    chunk = 1024
    deep = ins[0].shape[0] * 16
    gu = dh = None
    for k in range(0, width, chunk):
        tok = jnp.concatenate([r[:, 0, :, k : k + chunk].reshape(deep, chunk) for r in ins])
        cot = jnp.concatenate([r[:, 1, :, k : k + chunk].reshape(deep, chunk) for r in ins])
        both = jnp.concatenate([wg_ref[k : k + chunk, :], wu_ref[k : k + chunk, :]], axis=1)
        one = jnp.dot(tok, both, preferred_element_type=jnp.float32)
        two = lax.dot_general(
            cot,
            wd_ref[:, k : k + chunk],
            (((1,), (1,)), ((), ())),
            preferred_element_type=jnp.float32,
        )
        gu, dh = (one, two) if gu is None else (gu + one, dh + two)
    gate, upper = gu[:, :hidden], gu[:, hidden:]
    s = jax.nn.sigmoid(gate)
    hid = (gate * s * upper).astype(jnp.bfloat16)
    dgate = (dh * upper * s * (1.0 + gate * (1.0 - s))).astype(jnp.bfloat16)
    dup = (dh * gate * s).astype(jnp.bfloat16)
    dgu = jnp.concatenate([dgate, dup], axis=1)
    for k in range(0, width, chunk):
        both = jnp.concatenate([wg_ref[k : k + chunk, :], wu_ref[k : k + chunk, :]], axis=1)
        out = jnp.dot(hid, wd_ref[:, k : k + chunk], preferred_element_type=jnp.float32)
        din = lax.dot_general(
            dgu, both, (((1,), (1,)), ((), ())), preferred_element_type=jnp.float32
        )
        for i, ref in enumerate(outs):
            rows = slice(i * deep, (i + 1) * deep)
            ref[:, 0, :, k : k + chunk] = out[rows].astype(jnp.bfloat16).reshape(-1, 16, chunk)
            ref[:, 1, :, k : k + chunk] = din[rows].astype(jnp.bfloat16).reshape(-1, 16, chunk)


def experts(blocks, weights):
    number = len(blocks)
    width, hidden = weights[0].shape
    count = number * blocks[0].shape[0] * 16
    inside = pl.BlockSpec(memory_space=pltpu.VMEM)
    return pl.pallas_call(
        functools.partial(block_kernel, number),
        in_specs=[inside] * (number + 3),
        out_specs=[inside] * number,
        out_shape=[jax.ShapeDtypeStruct(b.shape, jnp.bfloat16) for b in blocks],
        compiler_params=pltpu.CompilerParams(vmem_limit_bytes=24 << 20),
        cost_estimate=pl.CostEstimate(
            flops=12 * count * width * hidden,
            bytes_accessed=(3 << 20) + 4 * count * width * 2,
            transcendentals=count * hidden,
        ),
    )(*blocks, *weights)


def add_kernel(groups, *refs):
    ins, outs = refs[: sum(groups)], refs[sum(groups) :]
    at = 0
    for number, out in zip(groups, outs):
        total = ins[at][...].astype(jnp.float32)
        for ref in ins[at + 1 : at + number]:
            total += ref[...].astype(jnp.float32)
        out[...] = total.astype(jnp.bfloat16)
        at += number


def added(*groups):
    flat = [block for group in groups for block in group]
    size = sum(block.size for block in flat)
    inside = pl.BlockSpec(memory_space=pltpu.VMEM)
    return pl.pallas_call(
        functools.partial(add_kernel, [len(group) for group in groups]),
        in_specs=[inside] * len(flat),
        out_specs=[inside] * len(groups),
        out_shape=[jax.ShapeDtypeStruct(group[0].shape, jnp.bfloat16) for group in groups],
        compiler_params=pltpu.CompilerParams(vmem_limit_bytes=24 << 20),
        cost_estimate=pl.CostEstimate(flops=size, bytes_accessed=3 * size, transcendentals=0),
    )(*flat)


def large_stage(block, weights):
    one, two = block[:2], block[2:]
    from_left_one, from_right_two = right(one), left(two)
    from_left_two, from_right_one = right(two), left(one)
    far_one, far_two = right(from_left_one), left(from_right_two)
    own = experts([block], weights)[0]
    to_left_one, to_left_two, to_right_one, to_right_two = experts(
        [from_left_one, from_left_two, from_right_one, from_right_two], weights
    )
    to_far_one, to_far_two = experts([far_one, far_two], weights)
    got_one, got_two = right(to_far_one), left(to_far_two)
    two_from_left, one_from_right = right(to_right_two), left(to_left_one)
    sum_one, sum_two = added([to_right_one, got_one], [to_left_two, got_two])
    one_from_left, two_from_right = right(sum_one), left(sum_two)
    one, two = added([own[:2], one_from_left, one_from_right], [own[2:], two_from_left, two_from_right])
    return jnp.concatenate([one, two])


def shards(tokens, cotangent, expert_id, gate_weight, up_weight, down_weight):
    core = lax.axis_index("c")
    my_expert = lax.axis_index("zh") * 2 + core
    count, width = tokens.shape
    earlier = (
        jnp.arange(count, dtype=jnp.int32)[:, None] > jnp.arange(count, dtype=jnp.int32)[None, :]
    )
    slot = jnp.sum(((expert_id[:, None] == expert_id[None, :]) & earlier).astype(jnp.int32), axis=1)
    positions = jnp.arange(SEND, dtype=jnp.int32)
    selector = ((expert_id[None, :] == my_expert) & (slot[None, :] == positions[:, None])).astype(
        jnp.bfloat16
    )
    own_rows = jnp.dot(selector, tokens, preferred_element_type=jnp.float32)
    own_grads = jnp.dot(selector, cotangent, preferred_element_type=jnp.float32)
    own = jnp.stack([own_rows, own_grads]).astype(jnp.bfloat16)

    first = mixed_groups("x")
    part = spread(own, "zl")
    part = jnp.swapaxes(part, 0, 1).reshape(2, 16, width)
    part = spread(part, AXES, first)
    part = large_stage(part, (gate_weight[0], up_weight[0], down_weight[0]))
    part = fold(part, AXES, first)
    part = jnp.swapaxes(part.reshape(2, 4, SEND, width), 0, 1)
    mine = fold(part, "zl")

    mine = spread(mine, "zh")
    other = lax.ppermute(mine, "c", [(0, 1), (1, 0)])

    def cells(c):
        expert = (jnp.arange(4, dtype=jnp.int32) * 2 + c)[:, None, None]
        return ((expert_id[None, None, :] == expert) & (slot[None, None, :] == positions[:, None])).astype(
            jnp.bfloat16
        ).reshape(16, count)

    def back(index):
        both = jnp.concatenate([mine[:, index].reshape(16, width), other[:, index].reshape(16, width)])
        table = jnp.concatenate([cells(core), cells(1 - core)])
        return lax.dot_general(
            table, both, (((0,), (0,)), ((), ())), preferred_element_type=jnp.float32
        ).astype(jnp.bfloat16)

    return (back(0), back(1))


def solution(mesh):
    fine = Mesh(mesh.devices.reshape(SIZES), AXES)
    tensor, expert = ("y", "zl", "x"), ("zh", "c")
    placed = (
        P(tensor, None),
        P(tensor, None),
        P(tensor),
        P(expert, None, tensor),
        P(expert, None, tensor),
        P(expert, tensor, None),
    )
    return jax.shard_map(
        shards,
        mesh=fine,
        in_specs=placed,
        out_specs=(P(tensor, None), P(tensor, None)),
        check_vma=False,
    )
```

```python
import functools

import jax
import jax.numpy as jnp
from jax import lax
from jax.experimental import pallas as pl
from jax.experimental.pallas import tpu as pltpu
from jax.sharding import Mesh, PartitionSpec as P

SEND = 4
AXES = ("zh", "c", "y", "zl", "x")
SIZES = (4, 2, 4, 4, 4)
INSIDE = pl.BlockSpec(memory_space=pltpu.VMEM)


def device(zh, c, y, zl, x):
    return (((zh * 2 + c) * 4 + y) * 4 + zl) * 4 + x


def mixed_groups(first):
    groups = []
    for zh in range(4):
        for c in range(2):
            for zl in range(4):
                for still in range(4):
                    if (c == 0) == (first == "x"):
                        groups.append([device(zh, c, still, zl, k) for k in range(4)])
                    else:
                        groups.append([device(zh, c, k, zl, still) for k in range(4)])
    return groups


def along(step):
    pairs = []
    for zh in range(4):
        for zl in range(4):
            for y in range(4):
                for x in range(4):
                    pairs.append((device(zh, 0, y, zl, x), device(zh, 0, (y + step) % 4, zl, x)))
                    pairs.append((device(zh, 1, y, zl, x), device(zh, 1, y, zl, (x + step) % 4)))
    return pairs


def right(block):
    return lax.ppermute(block, AXES, along(1))


def left(block):
    return lax.ppermute(block, AXES, along(3))


def block_kernel(number, *refs):
    ins, (wg_ref, wu_ref, wd_ref), outs = refs[:number], refs[number : number + 3], refs[number + 3 :]
    width, hidden = wg_ref.shape
    chunk = 1024
    deep = ins[0].shape[0] * 16
    gu = dh = None
    for k in range(0, width, chunk):
        tok = jnp.concatenate([r[:, 0, :, k : k + chunk].reshape(deep, chunk) for r in ins])
        cot = jnp.concatenate([r[:, 1, :, k : k + chunk].reshape(deep, chunk) for r in ins])
        both = jnp.concatenate([wg_ref[k : k + chunk, :], wu_ref[k : k + chunk, :]], axis=1)
        one = jnp.dot(tok, both, preferred_element_type=jnp.float32)
        two = lax.dot_general(
            cot,
            wd_ref[:, k : k + chunk],
            (((1,), (1,)), ((), ())),
            preferred_element_type=jnp.float32,
        )
        gu, dh = (one, two) if gu is None else (gu + one, dh + two)
    gate, upper = gu[:, :hidden], gu[:, hidden:]
    s = jax.nn.sigmoid(gate)
    hid = (gate * s * upper).astype(jnp.bfloat16)
    dgate = (dh * upper * s * (1.0 + gate * (1.0 - s))).astype(jnp.bfloat16)
    dup = (dh * gate * s).astype(jnp.bfloat16)
    dgu = jnp.concatenate([dgate, dup], axis=1)
    for k in range(0, width, chunk):
        both = jnp.concatenate([wg_ref[k : k + chunk, :], wu_ref[k : k + chunk, :]], axis=1)
        out = jnp.dot(hid, wd_ref[:, k : k + chunk], preferred_element_type=jnp.float32)
        din = lax.dot_general(
            dgu, both, (((1,), (1,)), ((), ())), preferred_element_type=jnp.float32
        )
        part = outs[0].shape[0] * 16
        for i, ref in enumerate(outs):
            rows = slice(i * part, (i + 1) * part)
            ref[:, 0, :, k : k + chunk] = out[rows].astype(jnp.bfloat16).reshape(-1, 16, chunk)
            ref[:, 1, :, k : k + chunk] = din[rows].astype(jnp.bfloat16).reshape(-1, 16, chunk)


def experts(blocks, weights):
    number = len(blocks)
    width, hidden = weights[0].shape
    count = number * blocks[0].shape[0] * 16
    return pl.pallas_call(
        functools.partial(block_kernel, number),
        in_specs=[INSIDE] * (number + 3),
        out_specs=[INSIDE] * (count // 32),
        out_shape=[jax.ShapeDtypeStruct((2,) + blocks[0].shape[1:], jnp.bfloat16)] * (count // 32),
        compiler_params=pltpu.CompilerParams(vmem_limit_bytes=24 << 20),
        cost_estimate=pl.CostEstimate(
            flops=12 * count * width * hidden,
            bytes_accessed=(3 << 20) + 4 * count * width * 2,
            transcendentals=count * hidden,
        ),
    )(*blocks, *weights)


def add_kernel(groups, *refs):
    ins, outs = refs[: sum(groups)], refs[sum(groups) :]
    at = 0
    for number, out in zip(groups, outs):
        total = ins[at][...].astype(jnp.float32)
        for ref in ins[at + 1 : at + number]:
            total += ref[...].astype(jnp.float32)
        out[...] = total.astype(out.dtype)
        at += number


def added(*groups):
    flat = [block for *group, _ in groups for block in group]
    size = sum(block.size for block in flat)
    return pl.pallas_call(
        functools.partial(add_kernel, [len(group) - 1 for group in groups]),
        in_specs=[INSIDE] * len(flat),
        out_specs=[INSIDE] * len(groups),
        out_shape=[jax.ShapeDtypeStruct(group[0].shape, group[-1]) for group in groups],
        compiler_params=pltpu.CompilerParams(vmem_limit_bytes=24 << 20),
        cost_estimate=pl.CostEstimate(flops=size, bytes_accessed=3 * size, transcendentals=0),
    )(*flat)


def join_kernel(*refs):
    ins, out = refs[:-1], refs[-1]
    half = ins[0].shape[0]
    for k in range(2):
        total = ins[2 * k][...].astype(jnp.float32) + ins[2 * k + 1][...].astype(jnp.float32)
        out[k * half : (k + 1) * half] = total.astype(out.dtype)


def light_kernel(got_ref, out_ref):
    for i in range(2):
        total = got_ref[0, i].astype(jnp.float32)
        for k in range(1, 4):
            total += got_ref[k, i].astype(jnp.float32)
        for z in range(4):
            out_ref[z, i] = total[4 * z : 4 * z + 4].astype(jnp.bfloat16)


def last_kernel(got_ref, out_ref):
    for i in range(2):
        total = got_ref[0, i].astype(jnp.float32)
        for k in range(1, 4):
            total += got_ref[k, i].astype(jnp.float32)
        out_ref[i] = total.astype(jnp.bfloat16)


def widen_kernel(got_ref, out_ref):
    for i in range(2):
        rows = jnp.concatenate([got_ref[z, i].astype(jnp.float32) for z in range(4)])
        rows = rows.astype(jnp.bfloat16)
        for k in range(4):
            out_ref[k, i] = rows


def columns_of(row):
    count = row.shape[1]
    at = lax.broadcasted_iota(jnp.int32, (count, count), 0)
    to = lax.broadcasted_iota(jnp.int32, (count, count), 1)
    return jnp.sum(jnp.where(at == to, row, 0), axis=1, keepdims=True)


def pick_kernel(id_ref, tokens_ref, grads_ref, out_ref):
    expert = lax.axis_index("zh") * 2 + lax.axis_index("c")
    row = id_ref[...]
    count = row.shape[1]
    at = lax.broadcasted_iota(jnp.int32, (count, count), 0)
    to = lax.broadcasted_iota(jnp.int32, (count, count), 1)
    same = (columns_of(row) == row) & (at < to)
    slot = jnp.sum(same.astype(jnp.int32), axis=0, keepdims=True)
    place = jnp.where(row == expert, slot, -1)
    wanted = lax.broadcasted_iota(jnp.int32, (8, count), 0)
    table = (wanted == place).astype(jnp.float32).astype(jnp.bfloat16)
    for i, ref in enumerate((tokens_ref, grads_ref)):
        rows = jnp.dot(table, ref[...], preferred_element_type=jnp.float32)
        for k in range(4):
            out_ref[k, i] = rows[:SEND].astype(jnp.bfloat16)


def back_kernel(id_ref, got_ref, *outs):
    row = id_ref[...]
    count = row.shape[1]
    column = columns_of(row)
    at = lax.broadcasted_iota(jnp.int32, (count, count), 0)
    to = lax.broadcasted_iota(jnp.int32, (count, count), 1)
    same = (column == row) & (to < at)
    slot = jnp.sum(same.astype(jnp.int32), axis=1, keepdims=True)
    cells = got_ref.shape[0] * SEND
    place = column * SEND + slot
    table = lax.broadcasted_iota(jnp.int32, (count, cells), 1) == place
    table = table.astype(jnp.float32).astype(jnp.bfloat16)
    for i, out in enumerate(outs):
        rows = jnp.concatenate([got_ref[e, i].astype(jnp.float32) for e in range(got_ref.shape[0])])
        out[...] = jnp.dot(
            table, rows.astype(jnp.bfloat16), preferred_element_type=jnp.float32
        ).astype(jnp.bfloat16)


def small(kernel, shapes, *arrays):
    size = sum(array.size for array in arrays)
    return pl.pallas_call(
        kernel,
        in_specs=[INSIDE] * len(arrays),
        out_specs=jax.tree.map(lambda _: INSIDE, shapes),
        out_shape=jax.tree.map(lambda shape: jax.ShapeDtypeStruct(shape.shape, jnp.bfloat16), shapes),
        compiler_params=pltpu.CompilerParams(vmem_limit_bytes=24 << 20),
        cost_estimate=pl.CostEstimate(flops=size, bytes_accessed=3 * size, transcendentals=0),
    )(*arrays)


def like(*shape):
    return jax.ShapeDtypeStruct(shape, jnp.bfloat16)


def large_stage(block, weights):
    from_left, from_right = right(block), left(block)
    far_one, far_two = right(from_left[:2]), left(from_right[2:])
    own_one, own_two = experts([block], weights)
    left_one, left_two, right_one, right_two = experts([from_left, from_right], weights)
    far_one, far_two, left_one, left_two, right_one, right_two = lax.optimization_barrier(
        (far_one, far_two, left_one, left_two, right_one, right_two)
    )
    to_far_one, to_far_two = experts([far_one, far_two], weights)
    two_from_left, one_from_right = right(right_two), left(left_one)
    got_one, got_two = right(to_far_one), left(to_far_two)
    sum_one, sum_two, one, two = added(
        [right_one, got_one, jnp.bfloat16],
        [left_two, got_two, jnp.bfloat16],
        [own_one, one_from_right, jnp.float32],
        [own_two, two_from_left, jnp.float32],
    )
    one_from_left, two_from_right = right(sum_one), left(sum_two)
    return small(join_kernel, like(*block.shape), one, one_from_left, two, two_from_right)


def shards(tokens, cotangent, expert_id, gate_weight, up_weight, down_weight):
    count, width = tokens.shape
    ids = expert_id.reshape(1, count)
    first = mixed_groups("x")

    def exchange(blocks, axis, groups=None):
        return lax.all_to_all(blocks, axis, 0, 0, axis_index_groups=groups, tiled=True)

    part = exchange(small(pick_kernel, like(4, 2, SEND, width), ids, tokens, cotangent), "zl")
    part = exchange(small(widen_kernel, like(4, 2, 16, width), part), AXES, first)
    part = large_stage(part, (gate_weight[0], up_weight[0], down_weight[0]))
    part = exchange(part, AXES, first)
    part = exchange(small(light_kernel, like(4, 2, SEND, width), part), "zl")
    mine = small(last_kernel, like(2, SEND, width), part)
    every = lax.all_gather(mine, ("zh", "c"), axis=0)
    return tuple(small(back_kernel, [like(count, width)] * 2, ids, every))


def solution(mesh):
    fine = Mesh(mesh.devices.reshape(SIZES), AXES)
    tensor, expert = ("y", "zl", "x"), ("zh", "c")
    placed = (
        P(tensor, None),
        P(tensor, None),
        P(tensor),
        P(expert, None, tensor),
        P(expert, None, tensor),
        P(expert, tensor, None),
    )
    return jax.shard_map(
        shards,
        mesh=fine,
        in_specs=placed,
        out_specs=(P(tensor, None), P(tensor, None)),
        check_vma=False,
    )
```

```python
import functools

import jax
import jax.numpy as jnp
from jax import lax
from jax.experimental import pallas as pl
from jax.experimental.pallas import tpu as pltpu
from jax.sharding import Mesh, PartitionSpec as P

SEND = 4
AXES = ("zh", "c", "y", "zl", "x")
SIZES = (4, 2, 4, 4, 4)
INSIDE = pl.BlockSpec(memory_space=pltpu.VMEM)


def device(zh, c, y, zl, x):
    return (((zh * 2 + c) * 4 + y) * 4 + zl) * 4 + x


def mixed_groups(first):
    groups = []
    for zh in range(4):
        for c in range(2):
            for zl in range(4):
                for still in range(4):
                    if (c == 0) == (first == "x"):
                        groups.append([device(zh, c, still, zl, k) for k in range(4)])
                    else:
                        groups.append([device(zh, c, k, zl, still) for k in range(4)])
    return groups


def along(step):
    pairs = []
    for zh in range(4):
        for zl in range(4):
            for y in range(4):
                for x in range(4):
                    pairs.append((device(zh, 0, y, zl, x), device(zh, 0, (y + step) % 4, zl, x)))
                    pairs.append((device(zh, 1, y, zl, x), device(zh, 1, y, zl, (x + step) % 4)))
    return pairs


def right(block):
    return lax.ppermute(block, AXES, along(1))


def left(block):
    return lax.ppermute(block, AXES, along(3))


def block_kernel(number, after, *refs):
    ins, (wg_ref, wu_ref, wd_ref) = refs[:number], refs[number : number + 3]
    outs = refs[number + 3 + after :]
    width, hidden = wg_ref.shape
    chunk = 1024
    deep = ins[0].shape[0] * 16
    gu = dh = None
    for k in range(0, width, chunk):
        tok = jnp.concatenate([r[:, 0, :, k : k + chunk].reshape(deep, chunk) for r in ins])
        cot = jnp.concatenate([r[:, 1, :, k : k + chunk].reshape(deep, chunk) for r in ins])
        both = jnp.concatenate([wg_ref[k : k + chunk, :], wu_ref[k : k + chunk, :]], axis=1)
        one = jnp.dot(tok, both, preferred_element_type=jnp.float32)
        two = lax.dot_general(
            cot,
            wd_ref[:, k : k + chunk],
            (((1,), (1,)), ((), ())),
            preferred_element_type=jnp.float32,
        )
        gu, dh = (one, two) if gu is None else (gu + one, dh + two)
    gate, upper = gu[:, :hidden], gu[:, hidden:]
    s = jax.nn.sigmoid(gate)
    hid = (gate * s * upper).astype(jnp.bfloat16)
    dgate = (dh * upper * s * (1.0 + gate * (1.0 - s))).astype(jnp.bfloat16)
    dup = (dh * gate * s).astype(jnp.bfloat16)
    dgu = jnp.concatenate([dgate, dup], axis=1)
    for k in range(0, width, chunk):
        both = jnp.concatenate([wg_ref[k : k + chunk, :], wu_ref[k : k + chunk, :]], axis=1)
        out = jnp.dot(hid, wd_ref[:, k : k + chunk], preferred_element_type=jnp.float32)
        din = lax.dot_general(
            dgu, both, (((1,), (1,)), ((), ())), preferred_element_type=jnp.float32
        )
        part = outs[0].shape[0] * 16
        for i, ref in enumerate(outs):
            rows = slice(i * part, (i + 1) * part)
            ref[:, 0, :, k : k + chunk] = out[rows].astype(jnp.bfloat16).reshape(-1, 16, chunk)
            ref[:, 1, :, k : k + chunk] = din[rows].astype(jnp.bfloat16).reshape(-1, 16, chunk)


def experts(blocks, weights, after=()):
    number = len(blocks)
    width, hidden = weights[0].shape
    count = number * blocks[0].shape[0] * 16
    return pl.pallas_call(
        functools.partial(block_kernel, number, len(after)),
        in_specs=[INSIDE] * (number + 3) + [pl.BlockSpec(memory_space=pl.ANY)] * len(after),
        out_specs=[INSIDE] * (count // 32),
        out_shape=[jax.ShapeDtypeStruct((2,) + blocks[0].shape[1:], jnp.bfloat16)] * (count // 32),
        compiler_params=pltpu.CompilerParams(vmem_limit_bytes=24 << 20),
        cost_estimate=pl.CostEstimate(
            flops=12 * count * width * hidden,
            bytes_accessed=(3 << 20) + 4 * count * width * 2,
            transcendentals=count * hidden,
        ),
    )(*blocks, *weights, *after)


def add_kernel(groups, *refs):
    ins, outs = refs[: sum(groups)], refs[sum(groups) :]
    at = 0
    for number, out in zip(groups, outs):
        total = ins[at][...].astype(jnp.float32)
        for ref in ins[at + 1 : at + number]:
            total += ref[...].astype(jnp.float32)
        out[...] = total.astype(out.dtype)
        at += number


def added(*groups):
    flat = [block for *group, _ in groups for block in group]
    size = sum(block.size for block in flat)
    return pl.pallas_call(
        functools.partial(add_kernel, [len(group) - 1 for group in groups]),
        in_specs=[INSIDE] * len(flat),
        out_specs=[INSIDE] * len(groups),
        out_shape=[jax.ShapeDtypeStruct(group[0].shape, group[-1]) for group in groups],
        compiler_params=pltpu.CompilerParams(vmem_limit_bytes=24 << 20),
        cost_estimate=pl.CostEstimate(flops=size, bytes_accessed=3 * size, transcendentals=0),
    )(*flat)


def join_kernel(*refs):
    ins, out = refs[:-1], refs[-1]
    half = ins[0].shape[0]
    for k in range(2):
        total = ins[3 * k][...].astype(jnp.float32)
        for ref in ins[3 * k + 1 : 3 * k + 3]:
            total += ref[...].astype(jnp.float32)
        out[k * half : (k + 1) * half] = total.astype(out.dtype)


def light_kernel(got_ref, out_ref):
    for i in range(2):
        total = got_ref[0, i].astype(jnp.float32)
        for k in range(1, 4):
            total += got_ref[k, i].astype(jnp.float32)
        for z in range(4):
            out_ref[z, i] = total[4 * z : 4 * z + 4].astype(jnp.bfloat16)


def last_kernel(got_ref, out_ref):
    for i in range(2):
        total = got_ref[0, i].astype(jnp.float32)
        for k in range(1, 4):
            total += got_ref[k, i].astype(jnp.float32)
        out_ref[i] = total.astype(jnp.bfloat16)


def widen_kernel(got_ref, out_ref):
    for i in range(2):
        rows = jnp.concatenate([got_ref[z, i].astype(jnp.float32) for z in range(4)])
        rows = rows.astype(jnp.bfloat16)
        for k in range(4):
            out_ref[k, i] = rows


def columns_of(row):
    count = row.shape[1]
    at = lax.broadcasted_iota(jnp.int32, (count, count), 0)
    to = lax.broadcasted_iota(jnp.int32, (count, count), 1)
    return jnp.sum(jnp.where(at == to, row, 0), axis=1, keepdims=True)


def pick_kernel(id_ref, tokens_ref, grads_ref, out_ref):
    expert = lax.axis_index("zh") * 2 + lax.axis_index("c")
    row = id_ref[...]
    count = row.shape[1]
    at = lax.broadcasted_iota(jnp.int32, (count, count), 0)
    to = lax.broadcasted_iota(jnp.int32, (count, count), 1)
    same = (columns_of(row) == row) & (at < to)
    slot = jnp.sum(same.astype(jnp.int32), axis=0, keepdims=True)
    place = jnp.where(row == expert, slot, -1)
    wanted = lax.broadcasted_iota(jnp.int32, (8, count), 0)
    table = (wanted == place).astype(jnp.float32).astype(jnp.bfloat16)
    for i, ref in enumerate((tokens_ref, grads_ref)):
        rows = jnp.dot(table, ref[...], preferred_element_type=jnp.float32)
        for k in range(4):
            out_ref[k, i] = rows[:SEND].astype(jnp.bfloat16)


def back_kernel(id_ref, got_ref, *outs):
    row = id_ref[...]
    count = row.shape[1]
    column = columns_of(row)
    at = lax.broadcasted_iota(jnp.int32, (count, count), 0)
    to = lax.broadcasted_iota(jnp.int32, (count, count), 1)
    same = (column == row) & (to < at)
    slot = jnp.sum(same.astype(jnp.int32), axis=1, keepdims=True)
    cells = got_ref.shape[0] * SEND
    place = column * SEND + slot
    table = lax.broadcasted_iota(jnp.int32, (count, cells), 1) == place
    table = table.astype(jnp.float32).astype(jnp.bfloat16)
    for i, out in enumerate(outs):
        rows = jnp.concatenate([got_ref[e, i].astype(jnp.float32) for e in range(got_ref.shape[0])])
        out[...] = jnp.dot(
            table, rows.astype(jnp.bfloat16), preferred_element_type=jnp.float32
        ).astype(jnp.bfloat16)


def small(kernel, shapes, *arrays):
    size = sum(array.size for array in arrays)
    return pl.pallas_call(
        kernel,
        in_specs=[INSIDE] * len(arrays),
        out_specs=jax.tree.map(lambda _: INSIDE, shapes),
        out_shape=jax.tree.map(lambda shape: jax.ShapeDtypeStruct(shape.shape, jnp.bfloat16), shapes),
        compiler_params=pltpu.CompilerParams(vmem_limit_bytes=24 << 20),
        cost_estimate=pl.CostEstimate(flops=size, bytes_accessed=3 * size, transcendentals=0),
    )(*arrays)


def like(*shape):
    return jax.ShapeDtypeStruct(shape, jnp.bfloat16)


def large_stage(block, weights):
    one, two = block[:2], block[2:]
    from_left_one, from_right_two = right(one), left(two)
    from_left_two, from_right_one = right(two), left(one)
    far_one, far_two = right(from_left_one), left(from_right_two)
    own_one, own_two = experts([block], weights)
    left_one, left_two, right_one, right_two = experts(
        [from_left_one, from_left_two, from_right_one, from_right_two], weights
    )
    to_far_one, to_far_two = experts([far_one, far_two], weights, (right_two,))
    two_from_left, one_from_right = right(right_two), left(left_one)
    got_one, got_two = right(to_far_one), left(to_far_two)
    sum_one, sum_two = added(
        [right_one, got_one, jnp.bfloat16], [left_two, got_two, jnp.bfloat16]
    )
    one_from_left, two_from_right = right(sum_one), left(sum_two)
    return small(
        join_kernel,
        like(*block.shape),
        own_one, one_from_left, one_from_right, own_two, two_from_left, two_from_right,
    )


def shards(tokens, cotangent, expert_id, gate_weight, up_weight, down_weight):
    count, width = tokens.shape
    ids = expert_id.reshape(1, count)
    first = mixed_groups("x")

    def exchange(blocks, axis, groups=None):
        return lax.all_to_all(blocks, axis, 0, 0, axis_index_groups=groups, tiled=True)

    own = pl.pallas_call(
        pick_kernel,
        grid=(1,),
        in_specs=[
            pl.BlockSpec((1, count), lambda i: (0, 0)),
            pl.BlockSpec((count, width), lambda i: (0, 0)),
            pl.BlockSpec((count, width), lambda i: (0, 0)),
        ],
        out_specs=pl.BlockSpec((4, 2, SEND, width), lambda i: (0, 0, 0, 0)),
        out_shape=like(4, 2, SEND, width),
        compiler_params=pltpu.CompilerParams(vmem_limit_bytes=24 << 20),
    )(ids, tokens, cotangent)
    part = exchange(own, "zl")
    part = exchange(small(widen_kernel, like(4, 2, 16, width), part), AXES, first)
    part = large_stage(part, (gate_weight[0], up_weight[0], down_weight[0]))
    part = exchange(part, AXES, first)
    part = exchange(small(light_kernel, like(4, 2, SEND, width), part), "zl")
    mine = small(last_kernel, like(2, SEND, width), part)
    every = lax.all_gather(mine, ("zh", "c"), axis=0)
    return tuple(small(back_kernel, [like(count, width)] * 2, ids, every))


def solution(mesh):
    fine = Mesh(mesh.devices.reshape(SIZES), AXES)
    tensor, expert = ("y", "zl", "x"), ("zh", "c")
    placed = (
        P(tensor, None),
        P(tensor, None),
        P(tensor),
        P(expert, None, tensor),
        P(expert, None, tensor),
        P(expert, tensor, None),
    )
    return jax.shard_map(
        shards,
        mesh=fine,
        in_specs=placed,
        out_specs=(P(tensor, None), P(tensor, None)),
        check_vma=False,
    )
```

```python
import functools

import jax
import jax.numpy as jnp
from jax import lax
from jax.experimental import pallas as pl
from jax.experimental.pallas import tpu as pltpu
from jax.sharding import Mesh, PartitionSpec as P

SEND = 4
AXES = ("zh", "c", "y", "zl", "x")
SIZES = (4, 2, 4, 4, 4)
INSIDE = pl.BlockSpec(memory_space=pltpu.VMEM)


def device(zh, c, y, zl, x):
    return (((zh * 2 + c) * 4 + y) * 4 + zl) * 4 + x


def mixed_groups(first):
    groups = []
    for zh in range(4):
        for c in range(2):
            for zl in range(4):
                for still in range(4):
                    if (c == 0) == (first == "x"):
                        groups.append([device(zh, c, still, zl, k) for k in range(4)])
                    else:
                        groups.append([device(zh, c, k, zl, still) for k in range(4)])
    return groups


def ring_pairs(partner):
    pairs = []
    for zh in range(4):
        for zl in range(4):
            for p in range(4):
                for still in range(4):
                    q = partner(p)
                    pairs.append((device(zh, 0, p, zl, still), device(zh, 0, q, zl, still)))
                    pairs.append((device(zh, 1, still, zl, p), device(zh, 1, still, zl, q)))
    return pairs


def from_mate(array):
    return lax.ppermute(array, AXES, ring_pairs(lambda p: p ^ 1))


def from_other(array):
    return lax.ppermute(array, AXES, ring_pairs(lambda p: 3 - p))


def block_kernel(rows_ref, *refs):
    weights, out_ref = refs[:6], refs[-1]
    gates, ups, downs = weights[0::3], weights[1::3], weights[2::3]
    width, hidden = gates[0].shape
    chunk = 1024
    deep = rows_ref.shape[0] * 16
    pieces = range(0, width, chunk)
    gates_of, ups_of, dhids_of = [], [], []
    for wg_ref, wu_ref, wd_ref in zip(gates, ups, downs):
        gu = dh = None
        for k in pieces:
            tok = rows_ref[:, 0, :, k : k + chunk].reshape(deep, chunk)
            cot = rows_ref[:, 1, :, k : k + chunk].reshape(deep, chunk)
            both = jnp.concatenate([wg_ref[k : k + chunk, :], wu_ref[k : k + chunk, :]], axis=1)
            one = jnp.dot(tok, both, preferred_element_type=jnp.float32)
            two = lax.dot_general(
                cot,
                wd_ref[:, k : k + chunk],
                (((1,), (1,)), ((), ())),
                preferred_element_type=jnp.float32,
            )
            gu, dh = (one, two) if gu is None else (gu + one, dh + two)
        gates_of.append(gu[:, :hidden])
        ups_of.append(gu[:, hidden:])
        dhids_of.append(dh)
    gate = jnp.concatenate(gates_of, axis=1)
    upper = jnp.concatenate(ups_of, axis=1)
    dhid = jnp.concatenate(dhids_of, axis=1)
    s = jax.nn.sigmoid(gate)
    hid = (gate * s * upper).astype(jnp.bfloat16)
    dgate = (dhid * upper * s * (1.0 + gate * (1.0 - s))).astype(jnp.bfloat16)
    dup = (dhid * gate * s).astype(jnp.bfloat16)
    for k in pieces:
        cut = slice(k, k + chunk)
        down = jnp.concatenate([ref[:, cut] for ref in downs])
        out = jnp.dot(hid, down, preferred_element_type=jnp.float32)
        out_ref[:, 0, :, cut] = out.astype(jnp.bfloat16).reshape(-1, 16, chunk)
        din = None
        for rows, refs_of in ((dgate, gates), (dup, ups)):
            both = jnp.concatenate([ref[cut, :] for ref in refs_of], axis=1)
            one = lax.dot_general(
                rows, both, (((1,), (1,)), ((), ())), preferred_element_type=jnp.float32
            )
            din = one if din is None else din + one
        out_ref[:, 1, :, cut] = din.astype(jnp.bfloat16).reshape(-1, 16, chunk)


def experts(block, weights):
    width, hidden = weights[0].shape
    count = block.shape[0] * 16
    return pl.pallas_call(
        block_kernel,
        in_specs=[INSIDE] * 7,
        out_specs=INSIDE,
        out_shape=like(*block.shape),
        compiler_params=pltpu.CompilerParams(vmem_limit_bytes=24 << 20),
        cost_estimate=pl.CostEstimate(
            flops=24 * count * width * hidden,
            bytes_accessed=(6 << 20) + 8 * count * width,
            transcendentals=2 * count * hidden,
        ),
    )(block, *weights)


def add_kernel(one_ref, two_ref, out_ref):
    total = one_ref[...].astype(jnp.float32) + two_ref[...].astype(jnp.float32)
    out_ref[...] = total.astype(jnp.bfloat16)


def light_kernel(got_ref, out_ref):
    for i in range(2):
        total = got_ref[0, i].astype(jnp.float32)
        for k in range(1, 4):
            total += got_ref[k, i].astype(jnp.float32)
        for z in range(4):
            out_ref[z, i] = total[4 * z : 4 * z + 4].astype(jnp.bfloat16)


def last_kernel(got_ref, out_ref):
    for i in range(2):
        total = got_ref[0, i].astype(jnp.float32)
        for k in range(1, 4):
            total += got_ref[k, i].astype(jnp.float32)
        out_ref[i] = total.astype(jnp.bfloat16)


def widen_kernel(got_ref, _, out_ref):
    for i in range(2):
        rows = jnp.concatenate([got_ref[z, i].astype(jnp.float32) for z in range(4)])
        rows = rows.astype(jnp.bfloat16)
        for k in range(4):
            out_ref[k, i] = rows


def columns_of(row):
    count = row.shape[1]
    at = lax.broadcasted_iota(jnp.int32, (count, count), 0)
    to = lax.broadcasted_iota(jnp.int32, (count, count), 1)
    return jnp.sum(jnp.where(at == to, row, 0), axis=1, keepdims=True)


def pick_kernel(id_ref, tokens_ref, grads_ref, out_ref):
    expert = lax.axis_index("zh") * 2 + lax.axis_index("c")
    row = id_ref[...]
    count = row.shape[1]
    at = lax.broadcasted_iota(jnp.int32, (count, count), 0)
    to = lax.broadcasted_iota(jnp.int32, (count, count), 1)
    same = (columns_of(row) == row) & (at < to)
    slot = jnp.sum(same.astype(jnp.int32), axis=0, keepdims=True)
    place = jnp.where(row == expert, slot, -1)
    wanted = lax.broadcasted_iota(jnp.int32, (8, count), 0)
    table = (wanted == place).astype(jnp.float32).astype(jnp.bfloat16)
    for i, ref in enumerate((tokens_ref, grads_ref)):
        rows = jnp.dot(table, ref[...], preferred_element_type=jnp.float32)
        for k in range(4):
            out_ref[k, i] = rows[:SEND].astype(jnp.bfloat16)


def back_kernel(id_ref, got_ref, *outs):
    row = id_ref[...]
    count = row.shape[1]
    column = columns_of(row)
    at = lax.broadcasted_iota(jnp.int32, (count, count), 0)
    to = lax.broadcasted_iota(jnp.int32, (count, count), 1)
    same = (column == row) & (to < at)
    slot = jnp.sum(same.astype(jnp.int32), axis=1, keepdims=True)
    cells = got_ref.shape[0] * SEND
    place = column * SEND + slot
    table = lax.broadcasted_iota(jnp.int32, (count, cells), 1) == place
    table = table.astype(jnp.float32).astype(jnp.bfloat16)
    for i, out in enumerate(outs):
        rows = jnp.concatenate([got_ref[e, i].astype(jnp.float32) for e in range(got_ref.shape[0])])
        out[...] = jnp.dot(
            table, rows.astype(jnp.bfloat16), preferred_element_type=jnp.float32
        ).astype(jnp.bfloat16)


def small(kernel, shapes, *arrays, after=()):
    size = sum(array.size for array in arrays)
    return pl.pallas_call(
        kernel,
        in_specs=[INSIDE] * len(arrays) + [pl.BlockSpec(memory_space=pl.ANY)] * len(after),
        out_specs=jax.tree.map(lambda _: INSIDE, shapes),
        out_shape=jax.tree.map(lambda shape: jax.ShapeDtypeStruct(shape.shape, jnp.bfloat16), shapes),
        compiler_params=pltpu.CompilerParams(vmem_limit_bytes=24 << 20),
        cost_estimate=pl.CostEstimate(flops=size, bytes_accessed=3 * size, transcendentals=0),
    )(*arrays, *after)


def like(*shape):
    return jax.ShapeDtypeStruct(shape, jnp.bfloat16)


def large_stage(block, weights):
    other = from_other(block)
    to_other = experts(other, weights)
    got = from_other(to_other)
    own = experts(block, weights)
    return small(add_kernel, like(*block.shape), own, got)


def shards(tokens, cotangent, expert_id, gate_weight, up_weight, down_weight):
    count, width = tokens.shape
    ids = expert_id.reshape(1, count)
    first = mixed_groups("x")
    held = [gate_weight[0], up_weight[0], down_weight[0]]
    mates = [from_mate(weight) for weight in held]

    def exchange(blocks, axis, groups=None):
        return lax.all_to_all(blocks, axis, 0, 0, axis_index_groups=groups, tiled=True)

    own = pl.pallas_call(
        pick_kernel,
        grid=(1,),
        in_specs=[
            pl.BlockSpec((1, count), lambda i: (0, 0)),
            pl.BlockSpec((count, width), lambda i: (0, 0)),
            pl.BlockSpec((count, width), lambda i: (0, 0)),
        ],
        out_specs=pl.BlockSpec((4, 2, SEND, width), lambda i: (0, 0, 0, 0)),
        out_shape=like(4, 2, SEND, width),
        compiler_params=pltpu.CompilerParams(vmem_limit_bytes=24 << 20),
    )(ids, tokens, cotangent)
    part = exchange(own, "zl")
    part = small(widen_kernel, like(4, 2, 16, width), part, after=mates[:1])
    part, mates[1] = lax.optimization_barrier((exchange(part, AXES, first), mates[1]))
    part = large_stage(part, held + mates)
    part = exchange(part, AXES, first)
    part = exchange(small(light_kernel, like(4, 2, SEND, width), part), "zl")
    mine = small(last_kernel, like(2, SEND, width), part)
    every = lax.all_gather(mine, ("zh", "c"), axis=0)
    return tuple(small(back_kernel, [like(count, width)] * 2, ids, every))


def solution(mesh):
    fine = Mesh(mesh.devices.reshape(SIZES), AXES)
    tensor, expert = ("y", "zl", "x"), ("zh", "c")
    placed = (
        P(tensor, None),
        P(tensor, None),
        P(tensor),
        P(expert, None, tensor),
        P(expert, None, tensor),
        P(expert, tensor, None),
    )
    return jax.shard_map(
        shards,
        mesh=fine,
        in_specs=placed,
        out_specs=(P(tensor, None), P(tensor, None)),
        check_vma=False,
    )
```

```python
import functools

import jax
import jax.numpy as jnp
from jax import lax
from jax.experimental import pallas as pl
from jax.experimental.pallas import tpu as pltpu
from jax.sharding import Mesh, PartitionSpec as P

SEND = 4
AXES = ("zh", "c", "y", "zl", "x")
SIZES = (4, 2, 4, 4, 4)
INSIDE = pl.BlockSpec(memory_space=pltpu.VMEM)


def device(zh, c, y, zl, x):
    return (((zh * 2 + c) * 4 + y) * 4 + zl) * 4 + x


def mixed_groups(first):
    groups = []
    for zh in range(4):
        for c in range(2):
            for zl in range(4):
                for still in range(4):
                    if (c == 0) == (first == "x"):
                        groups.append([device(zh, c, still, zl, k) for k in range(4)])
                    else:
                        groups.append([device(zh, c, k, zl, still) for k in range(4)])
    return groups


def ring_pairs(partner):
    pairs = []
    for zh in range(4):
        for zl in range(4):
            for p in range(4):
                for still in range(4):
                    q = partner(p)
                    pairs.append((device(zh, 0, p, zl, still), device(zh, 0, q, zl, still)))
                    pairs.append((device(zh, 1, still, zl, p), device(zh, 1, still, zl, q)))
    return pairs


def from_mate(array):
    return lax.ppermute(array, AXES, ring_pairs(lambda p: p ^ 1))


def from_other(array):
    return lax.ppermute(array, AXES, ring_pairs(lambda p: 3 - p))


def block_kernel(rows_ref, *refs):
    weights, out_ref = refs[:6], refs[-1]
    gates, ups, downs = weights[0::3], weights[1::3], weights[2::3]
    width, hidden = gates[0].shape
    chunk = 1024
    deep = rows_ref.shape[0] * 16
    pieces = range(0, width, chunk)
    gates_of, ups_of, dhids_of = [], [], []
    for wg_ref, wu_ref, wd_ref in zip(gates, ups, downs):
        gu = dh = None
        for k in pieces:
            tok = rows_ref[:, 0, :, k : k + chunk].reshape(deep, chunk)
            cot = rows_ref[:, 1, :, k : k + chunk].reshape(deep, chunk)
            both = jnp.concatenate([wg_ref[k : k + chunk, :], wu_ref[k : k + chunk, :]], axis=1)
            one = jnp.dot(tok, both, preferred_element_type=jnp.float32)
            two = lax.dot_general(
                cot,
                wd_ref[:, k : k + chunk],
                (((1,), (1,)), ((), ())),
                preferred_element_type=jnp.float32,
            )
            gu, dh = (one, two) if gu is None else (gu + one, dh + two)
        gates_of.append(gu[:, :hidden])
        ups_of.append(gu[:, hidden:])
        dhids_of.append(dh)
    gate = jnp.concatenate(gates_of, axis=1)
    upper = jnp.concatenate(ups_of, axis=1)
    dhid = jnp.concatenate(dhids_of, axis=1)
    s = jax.nn.sigmoid(gate)
    hid = (gate * s * upper).astype(jnp.bfloat16)
    dgate = (dhid * upper * s * (1.0 + gate * (1.0 - s))).astype(jnp.bfloat16)
    dup = (dhid * gate * s).astype(jnp.bfloat16)
    for k in pieces:
        cut = slice(k, k + chunk)
        down = jnp.concatenate([ref[:, cut] for ref in downs])
        out = jnp.dot(hid, down, preferred_element_type=jnp.float32)
        out_ref[:, 0, :, cut] = out.astype(jnp.bfloat16).reshape(-1, 16, chunk)
        din = None
        for rows, refs_of in ((dgate, gates), (dup, ups)):
            both = jnp.concatenate([ref[cut, :] for ref in refs_of], axis=1)
            one = lax.dot_general(
                rows, both, (((1,), (1,)), ((), ())), preferred_element_type=jnp.float32
            )
            din = one if din is None else din + one
        out_ref[:, 1, :, cut] = din.astype(jnp.bfloat16).reshape(-1, 16, chunk)


def experts(block, weights):
    width, hidden = weights[0].shape
    count = block.shape[0] * 16
    return pl.pallas_call(
        block_kernel,
        in_specs=[INSIDE] * 7,
        out_specs=INSIDE,
        out_shape=like(*block.shape),
        compiler_params=pltpu.CompilerParams(vmem_limit_bytes=24 << 20),
        cost_estimate=pl.CostEstimate(
            flops=24 * count * width * hidden,
            bytes_accessed=(6 << 20) + 8 * count * width,
            transcendentals=2 * count * hidden,
        ),
    )(block, *weights)


def rows_kernel(got_ref, _, out_ref):
    for i in range(2):
        rows = jnp.concatenate([got_ref[z, i].astype(jnp.float32) for z in range(4)])
        out_ref[i] = rows.astype(jnp.bfloat16)


def widen_kernel(own_ref, other_ref, _, out_ref):
    for k in range(4):
        out_ref[k, 0] = own_ref[...]
        out_ref[k, 1] = other_ref[...]


def light_kernel(got_ref, own_ref, other_ref):
    for i, out_ref in enumerate((own_ref, other_ref)):
        total = got_ref[0, i].astype(jnp.float32)
        for k in range(1, 4):
            total += got_ref[k, i].astype(jnp.float32)
        out_ref[...] = total.astype(out_ref.dtype)


def pair_kernel(own_ref, got_ref, out_ref):
    for i in range(2):
        total = own_ref[i].astype(jnp.float32) + got_ref[i].astype(jnp.float32)
        for z in range(4):
            out_ref[z, i] = total[4 * z : 4 * z + 4].astype(jnp.bfloat16)


def last_kernel(got_ref, out_ref):
    for i in range(2):
        total = got_ref[0, i].astype(jnp.float32)
        for k in range(1, 4):
            total += got_ref[k, i].astype(jnp.float32)
        out_ref[i] = total.astype(jnp.bfloat16)


def columns_of(row):
    count = row.shape[1]
    at = lax.broadcasted_iota(jnp.int32, (count, count), 0)
    to = lax.broadcasted_iota(jnp.int32, (count, count), 1)
    return jnp.sum(jnp.where(at == to, row, 0), axis=1, keepdims=True)


def pick_kernel(id_ref, tokens_ref, grads_ref, out_ref):
    expert = lax.axis_index("zh") * 2 + lax.axis_index("c")
    row = id_ref[...]
    count = row.shape[1]
    at = lax.broadcasted_iota(jnp.int32, (count, count), 0)
    to = lax.broadcasted_iota(jnp.int32, (count, count), 1)
    same = (columns_of(row) == row) & (at < to)
    slot = jnp.sum(same.astype(jnp.int32), axis=0, keepdims=True)
    place = jnp.where(row == expert, slot, -1)
    wanted = lax.broadcasted_iota(jnp.int32, (8, count), 0)
    table = (wanted == place).astype(jnp.float32).astype(jnp.bfloat16)
    for i, ref in enumerate((tokens_ref, grads_ref)):
        rows = jnp.dot(table, ref[...], preferred_element_type=jnp.float32)
        for k in range(4):
            out_ref[k, i] = rows[:SEND].astype(jnp.bfloat16)


def back_kernel(id_ref, got_ref, *outs):
    row = id_ref[...]
    count = row.shape[1]
    column = columns_of(row)
    at = lax.broadcasted_iota(jnp.int32, (count, count), 0)
    to = lax.broadcasted_iota(jnp.int32, (count, count), 1)
    same = (column == row) & (to < at)
    slot = jnp.sum(same.astype(jnp.int32), axis=1, keepdims=True)
    cells = got_ref.shape[0] * SEND
    place = column * SEND + slot
    table = lax.broadcasted_iota(jnp.int32, (count, cells), 1) == place
    table = table.astype(jnp.float32).astype(jnp.bfloat16)
    for i, out in enumerate(outs):
        rows = jnp.concatenate([got_ref[e, i].astype(jnp.float32) for e in range(got_ref.shape[0])])
        out[...] = jnp.dot(
            table, rows.astype(jnp.bfloat16), preferred_element_type=jnp.float32
        ).astype(jnp.bfloat16)


def small(kernel, shapes, *arrays, after=()):
    size = sum(array.size for array in arrays)
    return pl.pallas_call(
        kernel,
        in_specs=[INSIDE] * len(arrays) + [pl.BlockSpec(memory_space=pl.ANY)] * len(after),
        out_specs=jax.tree.map(lambda _: INSIDE, shapes),
        out_shape=shapes,
        compiler_params=pltpu.CompilerParams(vmem_limit_bytes=24 << 20),
        cost_estimate=pl.CostEstimate(flops=size, bytes_accessed=3 * size, transcendentals=0),
    )(*arrays, *after)


def like(*shape):
    return jax.ShapeDtypeStruct(shape, jnp.bfloat16)


def shards(tokens, cotangent, expert_id, gate_weight, up_weight, down_weight):
    count, width = tokens.shape
    ids = expert_id.reshape(1, count)
    first = mixed_groups("x")
    held = [gate_weight[0], up_weight[0], down_weight[0]]
    mates = [from_mate(weight) for weight in held]

    def exchange(blocks, axis, groups=None):
        return lax.all_to_all(blocks, axis, 0, 0, axis_index_groups=groups, tiled=True)

    own = pl.pallas_call(
        pick_kernel,
        grid=(1,),
        in_specs=[
            pl.BlockSpec((1, count), lambda i: (0, 0)),
            pl.BlockSpec((count, width), lambda i: (0, 0)),
            pl.BlockSpec((count, width), lambda i: (0, 0)),
        ],
        out_specs=pl.BlockSpec((4, 2, SEND, width), lambda i: (0, 0, 0, 0)),
        out_shape=like(4, 2, SEND, width),
        compiler_params=pltpu.CompilerParams(vmem_limit_bytes=24 << 20),
    )(ids, tokens, cotangent)
    part = exchange(own, "zl")
    block = small(rows_kernel, like(2, 16, width), part, after=mates[:1])
    part = small(
        widen_kernel, like(4, 2, 2, 16, width), block, from_other(block), after=mates[1:2]
    )
    part = exchange(part, AXES, first).reshape(8, 2, 16, width)
    part = experts(part, held + mates).reshape(4, 2, 2, 16, width)
    total = jax.ShapeDtypeStruct((2, 16, width), jnp.float32)
    own, other = small(light_kernel, [total, like(2, 16, width)], exchange(part, AXES, first))
    part = small(pair_kernel, like(4, 2, SEND, width), own, from_other(other))
    part = exchange(part, "zl")
    mine = small(last_kernel, like(2, SEND, width), part)
    every = lax.all_gather(mine, ("zh", "c"), axis=0)
    return tuple(small(back_kernel, [like(count, width)] * 2, ids, every))


def solution(mesh):
    fine = Mesh(mesh.devices.reshape(SIZES), AXES)
    tensor, expert = ("y", "zl", "x"), ("zh", "c")
    placed = (
        P(tensor, None),
        P(tensor, None),
        P(tensor),
        P(expert, None, tensor),
        P(expert, None, tensor),
        P(expert, tensor, None),
    )
    return jax.shard_map(
        shards,
        mesh=fine,
        in_specs=placed,
        out_specs=(P(tensor, None), P(tensor, None)),
        check_vma=False,
    )
```

```python
import functools

import jax
import jax.numpy as jnp
from jax import lax
from jax.experimental import pallas as pl
from jax.experimental.pallas import tpu as pltpu
from jax.sharding import Mesh, PartitionSpec as P

SEND = 4
AXES = ("zh", "c", "y", "zl", "x")
SIZES = (4, 2, 4, 4, 4)
SCRATCH = 4 << 20
INSIDE = pl.BlockSpec(memory_space=pltpu.VMEM)


def device(zh, c, y, zl, x):
    return (((zh * 2 + c) * 4 + y) * 4 + zl) * 4 + x


def mixed_groups(first):
    groups = []
    for zh in range(4):
        for c in range(2):
            for zl in range(4):
                for still in range(4):
                    if (c == 0) == (first == "x"):
                        groups.append([device(zh, c, still, zl, k) for k in range(4)])
                    else:
                        groups.append([device(zh, c, k, zl, still) for k in range(4)])
    return groups


def ring_pairs(partner):
    pairs = []
    for zh in range(4):
        for zl in range(4):
            for p in range(4):
                for still in range(4):
                    q = partner(p)
                    pairs.append((device(zh, 0, p, zl, still), device(zh, 0, q, zl, still)))
                    pairs.append((device(zh, 1, still, zl, p), device(zh, 1, still, zl, q)))
    return pairs


def from_mate(array):
    return lax.ppermute(array, AXES, ring_pairs(lambda p: p ^ 1))


def from_other(array):
    return lax.ppermute(array, AXES, ring_pairs(lambda p: 3 - p))


def block_kernel(rows_ref, *refs):
    weights, out_ref = refs[:6], refs[-1]
    gates, ups, downs = weights[0::3], weights[1::3], weights[2::3]
    width, hidden = gates[0].shape
    chunk = 1024
    deep = rows_ref.shape[0] * 16
    pieces = range(0, width, chunk)
    gates_of, ups_of, dhids_of = [], [], []
    for wg_ref, wu_ref, wd_ref in zip(gates, ups, downs):
        gu = dh = None
        for k in pieces:
            tok = rows_ref[:, 0, :, k : k + chunk].reshape(deep, chunk)
            cot = rows_ref[:, 1, :, k : k + chunk].reshape(deep, chunk)
            both = jnp.concatenate([wg_ref[k : k + chunk, :], wu_ref[k : k + chunk, :]], axis=1)
            one = jnp.dot(tok, both, preferred_element_type=jnp.float32)
            two = lax.dot_general(
                cot,
                wd_ref[:, k : k + chunk],
                (((1,), (1,)), ((), ())),
                preferred_element_type=jnp.float32,
            )
            gu, dh = (one, two) if gu is None else (gu + one, dh + two)
        gates_of.append(gu[:, :hidden])
        ups_of.append(gu[:, hidden:])
        dhids_of.append(dh)
    gate = jnp.concatenate(gates_of, axis=1)
    upper = jnp.concatenate(ups_of, axis=1)
    dhid = jnp.concatenate(dhids_of, axis=1)
    s = jax.nn.sigmoid(gate)
    hid = (gate * s * upper).astype(jnp.bfloat16)
    dgate = (dhid * upper * s * (1.0 + gate * (1.0 - s))).astype(jnp.bfloat16)
    dup = (dhid * gate * s).astype(jnp.bfloat16)
    for k in pieces:
        cut = slice(k, k + chunk)
        down = jnp.concatenate([ref[:, cut] for ref in downs])
        out = jnp.dot(hid, down, preferred_element_type=jnp.float32)
        out_ref[:, 0, :, cut] = out.astype(jnp.bfloat16).reshape(-1, 16, chunk)
        din = None
        for rows, refs_of in ((dgate, gates), (dup, ups)):
            both = jnp.concatenate([ref[cut, :] for ref in refs_of], axis=1)
            one = lax.dot_general(
                rows, both, (((1,), (1,)), ((), ())), preferred_element_type=jnp.float32
            )
            din = one if din is None else din + one
        out_ref[:, 1, :, cut] = din.astype(jnp.bfloat16).reshape(-1, 16, chunk)


def experts(block, weights):
    width, hidden = weights[0].shape
    count = block.shape[0] * 16
    return pl.pallas_call(
        block_kernel,
        in_specs=[INSIDE] * 7,
        out_specs=INSIDE,
        out_shape=like(*block.shape),
        compiler_params=pltpu.CompilerParams(vmem_limit_bytes=SCRATCH),
        cost_estimate=pl.CostEstimate(
            flops=24 * count * width * hidden,
            bytes_accessed=(6 << 20) + 8 * count * width,
            transcendentals=2 * count * hidden,
        ),
    )(block, *weights)


def rows_kernel(got_ref, _, out_ref):
    for i in range(2):
        rows = jnp.concatenate([got_ref[z, i].astype(jnp.float32) for z in range(4)])
        out_ref[i] = rows.astype(jnp.bfloat16)


def widen_kernel(own_ref, other_ref, _, out_ref):
    for k in range(4):
        out_ref[k, 0] = own_ref[...]
        out_ref[k, 1] = other_ref[...]


def light_kernel(got_ref, own_ref, other_ref):
    for i, out_ref in enumerate((own_ref, other_ref)):
        total = got_ref[0, i].astype(jnp.float32)
        for k in range(1, 4):
            total += got_ref[k, i].astype(jnp.float32)
        out_ref[...] = total.astype(out_ref.dtype)


def pair_kernel(own_ref, got_ref, out_ref):
    for i in range(2):
        total = own_ref[i].astype(jnp.float32) + got_ref[i].astype(jnp.float32)
        for z in range(4):
            out_ref[z, i] = total[4 * z : 4 * z + 4].astype(jnp.bfloat16)


def last_kernel(got_ref, out_ref):
    for i in range(2):
        total = got_ref[0, i].astype(jnp.float32)
        for k in range(1, 4):
            total += got_ref[k, i].astype(jnp.float32)
        out_ref[i] = total.astype(jnp.bfloat16)


def columns_of(row):
    count = row.shape[1]
    at = lax.broadcasted_iota(jnp.int32, (count, count), 0)
    to = lax.broadcasted_iota(jnp.int32, (count, count), 1)
    return jnp.sum(jnp.where(at == to, row, 0), axis=1, keepdims=True)


def pick_kernel(id_ref, tokens_ref, grads_ref, out_ref):
    expert = lax.axis_index("zh") * 2 + lax.axis_index("c")
    row = id_ref[...]
    count = row.shape[1]
    at = lax.broadcasted_iota(jnp.int32, (count, count), 0)
    to = lax.broadcasted_iota(jnp.int32, (count, count), 1)
    same = (columns_of(row) == row) & (at < to)
    slot = jnp.sum(same.astype(jnp.int32), axis=0, keepdims=True)
    place = jnp.where(row == expert, slot, -1)
    wanted = lax.broadcasted_iota(jnp.int32, (8, count), 0)
    table = (wanted == place).astype(jnp.float32).astype(jnp.bfloat16)
    for i, ref in enumerate((tokens_ref, grads_ref)):
        rows = jnp.dot(table, ref[...], preferred_element_type=jnp.float32)
        for k in range(4):
            out_ref[k, i] = rows[:SEND].astype(jnp.bfloat16)


def back_kernel(id_ref, got_ref, *outs):
    row = id_ref[...]
    count = row.shape[1]
    column = columns_of(row)
    at = lax.broadcasted_iota(jnp.int32, (count, count), 0)
    to = lax.broadcasted_iota(jnp.int32, (count, count), 1)
    same = (column == row) & (to < at)
    slot = jnp.sum(same.astype(jnp.int32), axis=1, keepdims=True)
    cells = got_ref.shape[0] * SEND
    place = column * SEND + slot
    table = lax.broadcasted_iota(jnp.int32, (count, cells), 1) == place
    table = table.astype(jnp.float32).astype(jnp.bfloat16)
    for i, out in enumerate(outs):
        rows = jnp.concatenate([got_ref[e, i].astype(jnp.float32) for e in range(got_ref.shape[0])])
        out[...] = jnp.dot(
            table, rows.astype(jnp.bfloat16), preferred_element_type=jnp.float32
        ).astype(jnp.bfloat16)


def small(kernel, shapes, *arrays, after=()):
    size = sum(array.size for array in arrays)
    return pl.pallas_call(
        kernel,
        in_specs=[INSIDE] * len(arrays) + [pl.BlockSpec(memory_space=pl.ANY)] * len(after),
        out_specs=jax.tree.map(lambda _: INSIDE, shapes),
        out_shape=shapes,
        compiler_params=pltpu.CompilerParams(vmem_limit_bytes=SCRATCH),
        cost_estimate=pl.CostEstimate(flops=size, bytes_accessed=3 * size, transcendentals=0),
    )(*arrays, *after)


def like(*shape):
    return jax.ShapeDtypeStruct(shape, jnp.bfloat16)


def shards(tokens, cotangent, expert_id, gate_weight, up_weight, down_weight):
    count, width = tokens.shape
    ids = expert_id.reshape(1, count)
    first = mixed_groups("x")
    held = [gate_weight[0], up_weight[0], down_weight[0]]
    mates = [from_mate(weight) for weight in held]

    def exchange(blocks, axis, groups=None):
        return lax.all_to_all(blocks, axis, 0, 0, axis_index_groups=groups, tiled=True)

    own = pl.pallas_call(
        pick_kernel,
        grid=(1,),
        in_specs=[
            pl.BlockSpec((1, count), lambda i: (0, 0)),
            pl.BlockSpec((count, width), lambda i: (0, 0)),
            pl.BlockSpec((count, width), lambda i: (0, 0)),
        ],
        out_specs=pl.BlockSpec((4, 2, SEND, width), lambda i: (0, 0, 0, 0)),
        out_shape=like(4, 2, SEND, width),
        compiler_params=pltpu.CompilerParams(vmem_limit_bytes=SCRATCH),
    )(ids, tokens, cotangent)
    part = exchange(own, "zl")
    block = small(rows_kernel, like(2, 16, width), part, after=mates[:1])
    part = small(
        widen_kernel, like(4, 2, 2, 16, width), block, from_other(block), after=mates[1:2]
    )
    part = exchange(part, AXES, first).reshape(8, 2, 16, width)
    part = experts(part, held + mates).reshape(4, 2, 2, 16, width)
    total = jax.ShapeDtypeStruct((2, 16, width), jnp.float32)
    own, other = small(light_kernel, [total, like(2, 16, width)], exchange(part, AXES, first))
    part = small(pair_kernel, like(4, 2, SEND, width), own, from_other(other))
    part = exchange(part, "zl")
    mine = small(last_kernel, like(2, SEND, width), part)
    every = lax.all_gather(mine, ("zh", "c"), axis=0)
    return tuple(small(back_kernel, [like(count, width)] * 2, ids, every))


def solution(mesh):
    fine = Mesh(mesh.devices.reshape(SIZES), AXES)
    tensor, expert = ("y", "zl", "x"), ("zh", "c")
    placed = (
        P(tensor, None),
        P(tensor, None),
        P(tensor),
        P(expert, None, tensor),
        P(expert, None, tensor),
        P(expert, tensor, None),
    )
    return jax.shard_map(
        shards,
        mesh=fine,
        in_specs=placed,
        out_specs=(P(tensor, None), P(tensor, None)),
        check_vma=False,
    )
```

```python
import functools

import jax
import jax.numpy as jnp
from jax import lax
from jax.experimental import pallas as pl
from jax.experimental.pallas import tpu as pltpu
from jax.sharding import Mesh, PartitionSpec as P

SEND = 4
AXES = ("zh", "c", "y", "zl", "x")
SIZES = (4, 2, 4, 4, 4)
SCRATCH = 4 << 20
INSIDE = pl.BlockSpec(memory_space=pltpu.VMEM)


def device(zh, c, y, zl, x):
    return (((zh * 2 + c) * 4 + y) * 4 + zl) * 4 + x


def mixed_groups(first):
    groups = []
    for zh in range(4):
        for c in range(2):
            for zl in range(4):
                for still in range(4):
                    if (c == 0) == (first == "x"):
                        groups.append([device(zh, c, still, zl, k) for k in range(4)])
                    else:
                        groups.append([device(zh, c, k, zl, still) for k in range(4)])
    return groups


def ring_pairs(partner):
    pairs = []
    for zh in range(4):
        for zl in range(4):
            for p in range(4):
                for still in range(4):
                    q = partner(p)
                    pairs.append((device(zh, 0, p, zl, still), device(zh, 0, q, zl, still)))
                    pairs.append((device(zh, 1, still, zl, p), device(zh, 1, still, zl, q)))
    return pairs


def from_mate(array):
    return lax.ppermute(array, AXES, ring_pairs(lambda p: p ^ 1))


def from_other(array):
    return lax.ppermute(array, AXES, ring_pairs(lambda p: 3 - p))


def block_kernel(rows_ref, *refs):
    weights, out_ref, tall, wide, sems = refs[:6], refs[6], refs[7], refs[8], refs[9]
    places = [tall.at[0], tall.at[1], wide.at[0], tall.at[2], tall.at[3], wide.at[1]]
    copies = [
        pltpu.make_async_copy(ref, place, sems.at[i])
        for i, (ref, place) in enumerate(zip(weights, places))
    ]
    for copy in copies:
        copy.start()
    gates, ups, downs = places[0::3], places[1::3], places[2::3]
    width, hidden = tall.shape[1:]
    chunk = 1024
    deep = rows_ref.shape[0] * 16
    pieces = range(0, width, chunk)
    gates_of, ups_of, dhids_of = [], [], []
    for i, (wg_ref, wu_ref, wd_ref) in enumerate(zip(gates, ups, downs)):
        for copy in copies[3 * i : 3 * i + 3]:
            copy.wait()
        gu = dh = None
        for k in pieces:
            tok = rows_ref[:, 0, :, k : k + chunk].reshape(deep, chunk)
            cot = rows_ref[:, 1, :, k : k + chunk].reshape(deep, chunk)
            both = jnp.concatenate([wg_ref[k : k + chunk, :], wu_ref[k : k + chunk, :]], axis=1)
            one = jnp.dot(tok, both, preferred_element_type=jnp.float32)
            two = lax.dot_general(
                cot,
                wd_ref[:, k : k + chunk],
                (((1,), (1,)), ((), ())),
                preferred_element_type=jnp.float32,
            )
            gu, dh = (one, two) if gu is None else (gu + one, dh + two)
        gates_of.append(gu[:, :hidden])
        ups_of.append(gu[:, hidden:])
        dhids_of.append(dh)
    gate = jnp.concatenate(gates_of, axis=1)
    upper = jnp.concatenate(ups_of, axis=1)
    dhid = jnp.concatenate(dhids_of, axis=1)
    s = jax.nn.sigmoid(gate)
    hid = (gate * s * upper).astype(jnp.bfloat16)
    dgate = (dhid * upper * s * (1.0 + gate * (1.0 - s))).astype(jnp.bfloat16)
    dup = (dhid * gate * s).astype(jnp.bfloat16)
    for k in pieces:
        cut = slice(k, k + chunk)
        down = jnp.concatenate([ref[:, cut] for ref in downs])
        out = jnp.dot(hid, down, preferred_element_type=jnp.float32)
        out_ref[:, 0, :, cut] = out.astype(jnp.bfloat16).reshape(-1, 16, chunk)
        din = None
        for rows, refs_of in ((dgate, gates), (dup, ups)):
            both = jnp.concatenate([ref[cut, :] for ref in refs_of], axis=1)
            one = lax.dot_general(
                rows, both, (((1,), (1,)), ((), ())), preferred_element_type=jnp.float32
            )
            din = one if din is None else din + one
        out_ref[:, 1, :, cut] = din.astype(jnp.bfloat16).reshape(-1, 16, chunk)


def experts(block, weights):
    width, hidden = weights[0].shape
    count = block.shape[0] * 16
    return pl.pallas_call(
        block_kernel,
        in_specs=[INSIDE] + [pl.BlockSpec(memory_space=pl.ANY)] * 6,
        out_specs=INSIDE,
        out_shape=like(*block.shape),
        scratch_shapes=[
            pltpu.VMEM((4, width, hidden), jnp.bfloat16),
            pltpu.VMEM((2, hidden, width), jnp.bfloat16),
            pltpu.SemaphoreType.DMA((6,)),
        ],
        compiler_params=pltpu.CompilerParams(vmem_limit_bytes=58 << 20),
        cost_estimate=pl.CostEstimate(
            flops=24 * count * width * hidden,
            bytes_accessed=(6 << 20) + 8 * count * width,
            transcendentals=2 * count * hidden,
        ),
    )(block, *weights)


def rows_kernel(got_ref, _, out_ref):
    for i in range(2):
        rows = jnp.concatenate([got_ref[z, i].astype(jnp.float32) for z in range(4)])
        out_ref[i] = rows.astype(jnp.bfloat16)


def widen_kernel(own_ref, other_ref, _, out_ref):
    for k in range(4):
        out_ref[k, 0] = own_ref[...]
        out_ref[k, 1] = other_ref[...]


def light_kernel(got_ref, own_ref, other_ref):
    for i, out_ref in enumerate((own_ref, other_ref)):
        total = got_ref[0, i].astype(jnp.float32)
        for k in range(1, 4):
            total += got_ref[k, i].astype(jnp.float32)
        out_ref[...] = total.astype(out_ref.dtype)


def pair_kernel(own_ref, got_ref, out_ref):
    for i in range(2):
        total = own_ref[i].astype(jnp.float32) + got_ref[i].astype(jnp.float32)
        for z in range(4):
            out_ref[z, i] = total[4 * z : 4 * z + 4].astype(jnp.bfloat16)


def last_kernel(got_ref, out_ref):
    for i in range(2):
        total = got_ref[0, i].astype(jnp.float32)
        for k in range(1, 4):
            total += got_ref[k, i].astype(jnp.float32)
        out_ref[i] = total.astype(jnp.bfloat16)


def columns_of(row):
    count = row.shape[1]
    at = lax.broadcasted_iota(jnp.int32, (count, count), 0)
    to = lax.broadcasted_iota(jnp.int32, (count, count), 1)
    return jnp.sum(jnp.where(at == to, row, 0), axis=1, keepdims=True)


def pick_kernel(id_ref, tokens_ref, grads_ref, out_ref):
    expert = lax.axis_index("zh") * 2 + lax.axis_index("c")
    row = id_ref[...]
    count = row.shape[1]
    at = lax.broadcasted_iota(jnp.int32, (count, count), 0)
    to = lax.broadcasted_iota(jnp.int32, (count, count), 1)
    same = (columns_of(row) == row) & (at < to)
    slot = jnp.sum(same.astype(jnp.int32), axis=0, keepdims=True)
    place = jnp.where(row == expert, slot, -1)
    wanted = lax.broadcasted_iota(jnp.int32, (8, count), 0)
    table = (wanted == place).astype(jnp.float32).astype(jnp.bfloat16)
    for i, ref in enumerate((tokens_ref, grads_ref)):
        rows = jnp.dot(table, ref[...], preferred_element_type=jnp.float32)
        for k in range(4):
            out_ref[k, i] = rows[:SEND].astype(jnp.bfloat16)


def back_kernel(id_ref, got_ref, *outs):
    row = id_ref[...]
    count = row.shape[1]
    column = columns_of(row)
    at = lax.broadcasted_iota(jnp.int32, (count, count), 0)
    to = lax.broadcasted_iota(jnp.int32, (count, count), 1)
    same = (column == row) & (to < at)
    slot = jnp.sum(same.astype(jnp.int32), axis=1, keepdims=True)
    cells = got_ref.shape[0] * SEND
    place = column * SEND + slot
    table = lax.broadcasted_iota(jnp.int32, (count, cells), 1) == place
    table = table.astype(jnp.float32).astype(jnp.bfloat16)
    for i, out in enumerate(outs):
        rows = jnp.concatenate([got_ref[e, i].astype(jnp.float32) for e in range(got_ref.shape[0])])
        out[...] = jnp.dot(
            table, rows.astype(jnp.bfloat16), preferred_element_type=jnp.float32
        ).astype(jnp.bfloat16)


def small(kernel, shapes, *arrays, after=()):
    size = sum(array.size for array in arrays)
    return pl.pallas_call(
        kernel,
        in_specs=[INSIDE] * len(arrays) + [pl.BlockSpec(memory_space=pl.ANY)] * len(after),
        out_specs=jax.tree.map(lambda _: INSIDE, shapes),
        out_shape=shapes,
        compiler_params=pltpu.CompilerParams(vmem_limit_bytes=SCRATCH),
        cost_estimate=pl.CostEstimate(flops=size, bytes_accessed=3 * size, transcendentals=0),
    )(*arrays, *after)


def like(*shape):
    return jax.ShapeDtypeStruct(shape, jnp.bfloat16)


def shards(tokens, cotangent, expert_id, gate_weight, up_weight, down_weight):
    count, width = tokens.shape
    ids = expert_id.reshape(1, count)
    first = mixed_groups("x")
    held = [gate_weight[0], up_weight[0], down_weight[0]]
    mates = [from_mate(weight) for weight in held]

    def exchange(blocks, axis, groups=None):
        return lax.all_to_all(blocks, axis, 0, 0, axis_index_groups=groups, tiled=True)

    own = pl.pallas_call(
        pick_kernel,
        grid=(1,),
        in_specs=[
            pl.BlockSpec((1, count), lambda i: (0, 0)),
            pl.BlockSpec((count, width), lambda i: (0, 0)),
            pl.BlockSpec((count, width), lambda i: (0, 0)),
        ],
        out_specs=pl.BlockSpec((4, 2, SEND, width), lambda i: (0, 0, 0, 0)),
        out_shape=like(4, 2, SEND, width),
        compiler_params=pltpu.CompilerParams(vmem_limit_bytes=SCRATCH),
    )(ids, tokens, cotangent)
    part = exchange(own, "zl")
    block = small(rows_kernel, like(2, 16, width), part, after=mates[:1])
    part = small(
        widen_kernel, like(4, 2, 2, 16, width), block, from_other(block), after=mates[1:2]
    )
    part = exchange(part, AXES, first).reshape(8, 2, 16, width)
    part = experts(part, held + mates).reshape(4, 2, 2, 16, width)
    total = jax.ShapeDtypeStruct((2, 16, width), jnp.float32)
    own, other = small(light_kernel, [total, like(2, 16, width)], exchange(part, AXES, first))
    part = small(pair_kernel, like(4, 2, SEND, width), own, from_other(other))
    part = exchange(part, "zl")
    mine = small(last_kernel, like(2, SEND, width), part)
    every = lax.all_gather(mine, ("zh", "c"), axis=0)
    return tuple(small(back_kernel, [like(count, width)] * 2, ids, every))


def solution(mesh):
    fine = Mesh(mesh.devices.reshape(SIZES), AXES)
    tensor, expert = ("y", "zl", "x"), ("zh", "c")
    placed = (
        P(tensor, None),
        P(tensor, None),
        P(tensor),
        P(expert, None, tensor),
        P(expert, None, tensor),
        P(expert, tensor, None),
    )
    return jax.shard_map(
        shards,
        mesh=fine,
        in_specs=placed,
        out_specs=(P(tensor, None), P(tensor, None)),
        check_vma=False,
    )
```

```python
import functools

import jax
import jax.numpy as jnp
from jax import lax
from jax.experimental import pallas as pl
from jax.experimental.pallas import tpu as pltpu
from jax.sharding import Mesh, PartitionSpec as P

SEND = 4
AXES = ("zh", "c", "y", "zl", "x")
SIZES = (4, 2, 4, 4, 4)
SCRATCH = 4 << 20
INSIDE = pl.BlockSpec(memory_space=pltpu.VMEM)


def device(zh, c, y, zl, x):
    return (((zh * 2 + c) * 4 + y) * 4 + zl) * 4 + x


def mixed_groups(first):
    groups = []
    for zh in range(4):
        for c in range(2):
            for zl in range(4):
                for still in range(4):
                    if (c == 0) == (first == "x"):
                        groups.append([device(zh, c, still, zl, k) for k in range(4)])
                    else:
                        groups.append([device(zh, c, k, zl, still) for k in range(4)])
    return groups


def ring_pairs(partner):
    pairs = []
    for zh in range(4):
        for zl in range(4):
            for p in range(4):
                for still in range(4):
                    q = partner(p)
                    pairs.append((device(zh, 0, p, zl, still), device(zh, 0, q, zl, still)))
                    pairs.append((device(zh, 1, still, zl, p), device(zh, 1, still, zl, q)))
    return pairs


def from_mate(array):
    return lax.ppermute(array, AXES, ring_pairs(lambda p: p ^ 1))


def from_other(array):
    return lax.ppermute(array, AXES, ring_pairs(lambda p: 3 - p))


def block_kernel(from_ref, *refs):
    weights, to_ref, rows_ref, out_ref, tall, wide, sems, out_sems = refs[:6], *refs[6:]
    width, hidden = tall.shape[1:]
    chunk = 1024
    pieces = range(0, width, chunk)
    deep = rows_ref.shape[0] * 16
    coming = []
    for i, k in enumerate(pieces):
        cut = pl.ds(k, chunk)
        pairs = [(from_ref.at[:, :, :, cut], rows_ref.at[:, :, :, cut])]
        for n in range(2):
            gate, up, down = weights[3 * n : 3 * n + 3]
            pairs.append((gate.at[cut, :], tall.at[2 * n, cut, :]))
            pairs.append((up.at[cut, :], tall.at[2 * n + 1, cut, :]))
            pairs.append((down.at[:, cut], wide.at[n, :, cut]))
        copies = [
            pltpu.make_async_copy(one, two, sems.at[i, n]) for n, (one, two) in enumerate(pairs)
        ]
        for copy in copies:
            copy.start()
        coming.append(copies)
    gu, dh = [None, None], [None, None]
    for copies, k in zip(coming, pieces):
        for copy in copies:
            copy.wait()
        tok = rows_ref[:, 0, :, k : k + chunk].reshape(deep, chunk)
        cot = rows_ref[:, 1, :, k : k + chunk].reshape(deep, chunk)
        for n in range(2):
            both = jnp.concatenate(
                [tall[2 * n, k : k + chunk, :], tall[2 * n + 1, k : k + chunk, :]], axis=1
            )
            one = jnp.dot(tok, both, preferred_element_type=jnp.float32)
            two = lax.dot_general(
                cot,
                wide[n, :, k : k + chunk],
                (((1,), (1,)), ((), ())),
                preferred_element_type=jnp.float32,
            )
            gu[n] = one if gu[n] is None else gu[n] + one
            dh[n] = two if dh[n] is None else dh[n] + two
    gate = jnp.concatenate([part[:, :hidden] for part in gu], axis=1)
    upper = jnp.concatenate([part[:, hidden:] for part in gu], axis=1)
    dhid = jnp.concatenate(dh, axis=1)
    s = jax.nn.sigmoid(gate)
    hid = (gate * s * upper).astype(jnp.bfloat16)
    dgate = (dhid * upper * s * (1.0 + gate * (1.0 - s))).astype(jnp.bfloat16)
    dup = (dhid * gate * s).astype(jnp.bfloat16)
    going = []
    for i, k in enumerate(pieces):
        cut = slice(k, k + chunk)
        down = jnp.concatenate([wide[n, :, cut] for n in range(2)])
        out = jnp.dot(hid, down, preferred_element_type=jnp.float32)
        out_ref[:, 0, :, cut] = out.astype(jnp.bfloat16).reshape(-1, 16, chunk)
        din = None
        for m, rows in enumerate((dgate, dup)):
            both = jnp.concatenate([tall[m, cut, :], tall[2 + m, cut, :]], axis=1)
            one = lax.dot_general(
                rows, both, (((1,), (1,)), ((), ())), preferred_element_type=jnp.float32
            )
            din = one if din is None else din + one
        out_ref[:, 1, :, cut] = din.astype(jnp.bfloat16).reshape(-1, 16, chunk)
        place = pl.ds(k, chunk)
        copy = pltpu.make_async_copy(
            out_ref.at[:, :, :, place], to_ref.at[:, :, :, place], out_sems.at[i]
        )
        copy.start()
        going.append(copy)
    for copy in going:
        copy.wait()


def experts(block, weights):
    width, hidden = weights[0].shape
    count = block.shape[0] * 16
    outside = pl.BlockSpec(memory_space=pl.ANY)
    return pl.pallas_call(
        block_kernel,
        in_specs=[outside] * 7,
        out_specs=outside,
        out_shape=like(*block.shape),
        scratch_shapes=[
            pltpu.VMEM(block.shape, jnp.bfloat16),
            pltpu.VMEM(block.shape, jnp.bfloat16),
            pltpu.VMEM((4, width, hidden), jnp.bfloat16),
            pltpu.VMEM((2, hidden, width), jnp.bfloat16),
            pltpu.SemaphoreType.DMA((width // 1024, 7)),
            pltpu.SemaphoreType.DMA((width // 1024,)),
        ],
        compiler_params=pltpu.CompilerParams(vmem_limit_bytes=58 << 20),
        cost_estimate=pl.CostEstimate(
            flops=24 * count * width * hidden,
            bytes_accessed=(6 << 20) + 8 * count * width,
            transcendentals=2 * count * hidden,
        ),
    )(block, *weights)


def rows_kernel(got_ref, _, out_ref):
    for i in range(2):
        rows = jnp.concatenate([got_ref[z, i].astype(jnp.float32) for z in range(4)])
        out_ref[i] = rows.astype(jnp.bfloat16)


def widen_kernel(own_ref, other_ref, _, out_ref):
    for k in range(4):
        out_ref[k, 0] = own_ref[...]
        out_ref[k, 1] = other_ref[...]


def light_kernel(got_ref, own_ref, other_ref):
    for i, out_ref in enumerate((own_ref, other_ref)):
        total = got_ref[0, i].astype(jnp.float32)
        for k in range(1, 4):
            total += got_ref[k, i].astype(jnp.float32)
        out_ref[...] = total.astype(out_ref.dtype)


def pair_kernel(own_ref, got_ref, out_ref):
    for i in range(2):
        total = own_ref[i].astype(jnp.float32) + got_ref[i].astype(jnp.float32)
        for z in range(4):
            out_ref[z, i] = total[4 * z : 4 * z + 4].astype(jnp.bfloat16)


def last_kernel(got_ref, out_ref):
    for i in range(2):
        total = got_ref[0, i].astype(jnp.float32)
        for k in range(1, 4):
            total += got_ref[k, i].astype(jnp.float32)
        out_ref[i] = total.astype(jnp.bfloat16)


def columns_of(row):
    count = row.shape[1]
    at = lax.broadcasted_iota(jnp.int32, (count, count), 0)
    to = lax.broadcasted_iota(jnp.int32, (count, count), 1)
    return jnp.sum(jnp.where(at == to, row, 0), axis=1, keepdims=True)


def pick_kernel(id_ref, tokens_ref, grads_ref, out_ref):
    expert = lax.axis_index("zh") * 2 + lax.axis_index("c")
    row = id_ref[...]
    count = row.shape[1]
    at = lax.broadcasted_iota(jnp.int32, (count, count), 0)
    to = lax.broadcasted_iota(jnp.int32, (count, count), 1)
    same = (columns_of(row) == row) & (at < to)
    slot = jnp.sum(same.astype(jnp.int32), axis=0, keepdims=True)
    place = jnp.where(row == expert, slot, -1)
    wanted = lax.broadcasted_iota(jnp.int32, (8, count), 0)
    table = (wanted == place).astype(jnp.float32).astype(jnp.bfloat16)
    for i, ref in enumerate((tokens_ref, grads_ref)):
        rows = jnp.dot(table, ref[...], preferred_element_type=jnp.float32)
        for k in range(4):
            out_ref[k, i] = rows[:SEND].astype(jnp.bfloat16)


def back_kernel(id_ref, got_ref, *outs):
    row = id_ref[...]
    count = row.shape[1]
    column = columns_of(row)
    at = lax.broadcasted_iota(jnp.int32, (count, count), 0)
    to = lax.broadcasted_iota(jnp.int32, (count, count), 1)
    same = (column == row) & (to < at)
    slot = jnp.sum(same.astype(jnp.int32), axis=1, keepdims=True)
    cells = got_ref.shape[0] * SEND
    place = column * SEND + slot
    table = lax.broadcasted_iota(jnp.int32, (count, cells), 1) == place
    table = table.astype(jnp.float32).astype(jnp.bfloat16)
    for i, out in enumerate(outs):
        rows = jnp.concatenate([got_ref[e, i].astype(jnp.float32) for e in range(got_ref.shape[0])])
        out[...] = jnp.dot(
            table, rows.astype(jnp.bfloat16), preferred_element_type=jnp.float32
        ).astype(jnp.bfloat16)


def small(kernel, shapes, *arrays, after=()):
    size = sum(array.size for array in arrays)
    return pl.pallas_call(
        kernel,
        in_specs=[INSIDE] * len(arrays) + [pl.BlockSpec(memory_space=pl.ANY)] * len(after),
        out_specs=jax.tree.map(lambda _: INSIDE, shapes),
        out_shape=shapes,
        compiler_params=pltpu.CompilerParams(vmem_limit_bytes=SCRATCH),
        cost_estimate=pl.CostEstimate(flops=size, bytes_accessed=3 * size, transcendentals=0),
    )(*arrays, *after)


def like(*shape):
    return jax.ShapeDtypeStruct(shape, jnp.bfloat16)


def shards(tokens, cotangent, expert_id, gate_weight, up_weight, down_weight):
    count, width = tokens.shape
    ids = expert_id.reshape(1, count)
    first = mixed_groups("x")
    held = [gate_weight[0], up_weight[0], down_weight[0]]
    mates = [from_mate(weight) for weight in held]

    def exchange(blocks, axis, groups=None):
        return lax.all_to_all(blocks, axis, 0, 0, axis_index_groups=groups, tiled=True)

    own = pl.pallas_call(
        pick_kernel,
        grid=(1,),
        in_specs=[
            pl.BlockSpec((1, count), lambda i: (0, 0)),
            pl.BlockSpec((count, width), lambda i: (0, 0)),
            pl.BlockSpec((count, width), lambda i: (0, 0)),
        ],
        out_specs=pl.BlockSpec((4, 2, SEND, width), lambda i: (0, 0, 0, 0)),
        out_shape=like(4, 2, SEND, width),
        compiler_params=pltpu.CompilerParams(vmem_limit_bytes=SCRATCH),
    )(ids, tokens, cotangent)
    part = exchange(own, "zl")
    block = small(rows_kernel, like(2, 16, width), part, after=mates[:1])
    part = small(
        widen_kernel, like(4, 2, 2, 16, width), block, from_other(block), after=mates[1:2]
    )
    part = exchange(part, AXES, first).reshape(8, 2, 16, width)
    part = experts(part, held + mates).reshape(4, 2, 2, 16, width)
    total = jax.ShapeDtypeStruct((2, 16, width), jnp.float32)
    own, other = small(light_kernel, [total, like(2, 16, width)], exchange(part, AXES, first))
    part = small(pair_kernel, like(4, 2, SEND, width), own, from_other(other))
    part = exchange(part, "zl")
    mine = small(last_kernel, like(2, SEND, width), part)
    every = lax.all_gather(mine, ("zh", "c"), axis=0)
    return tuple(small(back_kernel, [like(count, width)] * 2, ids, every))


def solution(mesh):
    fine = Mesh(mesh.devices.reshape(SIZES), AXES)
    tensor, expert = ("y", "zl", "x"), ("zh", "c")
    placed = (
        P(tensor, None),
        P(tensor, None),
        P(tensor),
        P(expert, None, tensor),
        P(expert, None, tensor),
        P(expert, tensor, None),
    )
    return jax.shard_map(
        shards,
        mesh=fine,
        in_specs=placed,
        out_specs=(P(tensor, None), P(tensor, None)),
        check_vma=False,
    )
```

```python
import functools

import jax
import jax.numpy as jnp
from jax import lax
from jax.experimental import pallas as pl
from jax.experimental.pallas import tpu as pltpu
from jax.sharding import Mesh, PartitionSpec as P

SEND = 4
AXES = ("zh", "c", "y", "zl", "x")
SIZES = (4, 2, 4, 4, 4)
SCRATCH = 4 << 20
INSIDE = pl.BlockSpec(memory_space=pltpu.VMEM)


def device(zh, c, y, zl, x):
    return (((zh * 2 + c) * 4 + y) * 4 + zl) * 4 + x


def mixed_groups(first):
    groups = []
    for zh in range(4):
        for c in range(2):
            for zl in range(4):
                for still in range(4):
                    if (c == 0) == (first == "x"):
                        groups.append([device(zh, c, still, zl, k) for k in range(4)])
                    else:
                        groups.append([device(zh, c, k, zl, still) for k in range(4)])
    return groups


def ring_pairs(partner):
    pairs = []
    for zh in range(4):
        for zl in range(4):
            for p in range(4):
                for still in range(4):
                    q = partner(p)
                    pairs.append((device(zh, 0, p, zl, still), device(zh, 0, q, zl, still)))
                    pairs.append((device(zh, 1, still, zl, p), device(zh, 1, still, zl, q)))
    return pairs


def from_mate(array):
    return lax.ppermute(array, AXES, ring_pairs(lambda p: p ^ 1))


def from_other(array):
    return lax.ppermute(array, AXES, ring_pairs(lambda p: 3 - p))


def block_kernel(rows_ref, *refs):
    weights, beside, out_ref = refs[:6], refs[6:-1], refs[-1]
    for ref in beside:
        out_ref[:, 0] = ref[...]
        out_ref = out_ref.at[:, 1]
    gates, ups, downs = weights[0::3], weights[1::3], weights[2::3]
    width, hidden = gates[0].shape
    chunk = 1024
    deep = rows_ref.shape[0] * 16
    pieces = range(0, width, chunk)
    gates_of, ups_of, dhids_of = [], [], []
    for wg_ref, wu_ref, wd_ref in zip(gates, ups, downs):
        gu = dh = None
        for k in pieces:
            tok = rows_ref[:, 0, :, k : k + chunk].reshape(deep, chunk)
            cot = rows_ref[:, 1, :, k : k + chunk].reshape(deep, chunk)
            both = jnp.concatenate([wg_ref[k : k + chunk, :], wu_ref[k : k + chunk, :]], axis=1)
            one = jnp.dot(tok, both, preferred_element_type=jnp.float32)
            two = lax.dot_general(
                cot,
                wd_ref[:, k : k + chunk],
                (((1,), (1,)), ((), ())),
                preferred_element_type=jnp.float32,
            )
            gu, dh = (one, two) if gu is None else (gu + one, dh + two)
        gates_of.append(gu[:, :hidden])
        ups_of.append(gu[:, hidden:])
        dhids_of.append(dh)
    gate = jnp.concatenate(gates_of, axis=1)
    upper = jnp.concatenate(ups_of, axis=1)
    dhid = jnp.concatenate(dhids_of, axis=1)
    s = jax.nn.sigmoid(gate)
    hid = (gate * s * upper).astype(jnp.bfloat16)
    dgate = (dhid * upper * s * (1.0 + gate * (1.0 - s))).astype(jnp.bfloat16)
    dup = (dhid * gate * s).astype(jnp.bfloat16)
    for k in pieces:
        cut = slice(k, k + chunk)
        down = jnp.concatenate([ref[:, cut] for ref in downs])
        out = jnp.dot(hid, down, preferred_element_type=jnp.float32)
        out_ref[:, 0, :, cut] = out.astype(jnp.bfloat16).reshape(-1, 16, chunk)
        din = None
        for rows, refs_of in ((dgate, gates), (dup, ups)):
            both = jnp.concatenate([ref[cut, :] for ref in refs_of], axis=1)
            one = lax.dot_general(
                rows, both, (((1,), (1,)), ((), ())), preferred_element_type=jnp.float32
            )
            din = one if din is None else din + one
        out_ref[:, 1, :, cut] = din.astype(jnp.bfloat16).reshape(-1, 16, chunk)


def experts(block, weights, *beside):
    width, hidden = weights[0].shape
    count = block.shape[0] * 16
    return pl.pallas_call(
        block_kernel,
        in_specs=[INSIDE] * (7 + len(beside)),
        out_specs=INSIDE,
        out_shape=like(4, *[2] * len(beside), *block.shape[1:]),
        compiler_params=pltpu.CompilerParams(vmem_limit_bytes=24 << 20),
        cost_estimate=pl.CostEstimate(
            flops=24 * count * width * hidden,
            bytes_accessed=(6 << 20) + 8 * count * width,
            transcendentals=2 * count * hidden,
        ),
    )(block, *weights, *beside)


def widen_kernel(got_ref, _, out_ref):
    for i in range(2):
        rows = jnp.concatenate([got_ref[z, i].astype(jnp.float32) for z in range(4)])
        rows = rows.astype(jnp.bfloat16)
        for k in range(4):
            out_ref[k, i] = rows


def light_kernel(got_ref, own_ref, other_ref):
    for i, out_ref in enumerate((own_ref, other_ref)):
        total = got_ref[0, i].astype(jnp.float32)
        for k in range(1, 4):
            total += got_ref[k, i].astype(jnp.float32)
        out_ref[...] = total.astype(out_ref.dtype)


def pair_kernel(own_ref, got_ref, out_ref):
    for i in range(2):
        total = own_ref[i].astype(jnp.float32) + got_ref[i].astype(jnp.float32)
        for z in range(4):
            out_ref[z, i] = total[4 * z : 4 * z + 4].astype(jnp.bfloat16)


def last_kernel(got_ref, out_ref):
    for i in range(2):
        total = got_ref[0, i].astype(jnp.float32)
        for k in range(1, 4):
            total += got_ref[k, i].astype(jnp.float32)
        out_ref[i] = total.astype(jnp.bfloat16)


def columns_of(row):
    count = row.shape[1]
    at = lax.broadcasted_iota(jnp.int32, (count, count), 0)
    to = lax.broadcasted_iota(jnp.int32, (count, count), 1)
    return jnp.sum(jnp.where(at == to, row, 0), axis=1, keepdims=True)


def pick_kernel(id_ref, tokens_ref, grads_ref, out_ref):
    expert = lax.axis_index("zh") * 2 + lax.axis_index("c")
    row = id_ref[...]
    count = row.shape[1]
    at = lax.broadcasted_iota(jnp.int32, (count, count), 0)
    to = lax.broadcasted_iota(jnp.int32, (count, count), 1)
    same = (columns_of(row) == row) & (at < to)
    slot = jnp.sum(same.astype(jnp.int32), axis=0, keepdims=True)
    place = jnp.where(row == expert, slot, -1)
    wanted = lax.broadcasted_iota(jnp.int32, (8, count), 0)
    table = (wanted == place).astype(jnp.float32).astype(jnp.bfloat16)
    for i, ref in enumerate((tokens_ref, grads_ref)):
        rows = jnp.dot(table, ref[...], preferred_element_type=jnp.float32)
        for k in range(4):
            out_ref[k, i] = rows[:SEND].astype(jnp.bfloat16)


def back_kernel(id_ref, got_ref, *outs):
    row = id_ref[...]
    count = row.shape[1]
    column = columns_of(row)
    at = lax.broadcasted_iota(jnp.int32, (count, count), 0)
    to = lax.broadcasted_iota(jnp.int32, (count, count), 1)
    same = (column == row) & (to < at)
    slot = jnp.sum(same.astype(jnp.int32), axis=1, keepdims=True)
    cells = got_ref.shape[0] * SEND
    place = column * SEND + slot
    table = lax.broadcasted_iota(jnp.int32, (count, cells), 1) == place
    table = table.astype(jnp.float32).astype(jnp.bfloat16)
    for i, out in enumerate(outs):
        rows = jnp.concatenate([got_ref[e, i].astype(jnp.float32) for e in range(got_ref.shape[0])])
        out[...] = jnp.dot(
            table, rows.astype(jnp.bfloat16), preferred_element_type=jnp.float32
        ).astype(jnp.bfloat16)


def small(kernel, shapes, *arrays, after=()):
    size = sum(array.size for array in arrays)
    return pl.pallas_call(
        kernel,
        in_specs=[INSIDE] * len(arrays) + [pl.BlockSpec(memory_space=pl.ANY)] * len(after),
        out_specs=jax.tree.map(lambda _: INSIDE, shapes),
        out_shape=shapes,
        compiler_params=pltpu.CompilerParams(vmem_limit_bytes=SCRATCH),
        cost_estimate=pl.CostEstimate(flops=size, bytes_accessed=3 * size, transcendentals=0),
    )(*arrays, *after)


def like(*shape):
    return jax.ShapeDtypeStruct(shape, jnp.bfloat16)


def shards(tokens, cotangent, expert_id, gate_weight, up_weight, down_weight):
    count, width = tokens.shape
    ids = expert_id.reshape(1, count)
    first = mixed_groups("x")
    held = [gate_weight[0], up_weight[0], down_weight[0]]
    mates = [from_mate(weight) for weight in held]

    def exchange(blocks, axis, groups=None):
        return lax.all_to_all(blocks, axis, 0, 0, axis_index_groups=groups, tiled=True)

    own = pl.pallas_call(
        pick_kernel,
        grid=(1,),
        in_specs=[
            pl.BlockSpec((1, count), lambda i: (0, 0)),
            pl.BlockSpec((count, width), lambda i: (0, 0)),
            pl.BlockSpec((count, width), lambda i: (0, 0)),
        ],
        out_specs=pl.BlockSpec((4, 2, SEND, width), lambda i: (0, 0, 0, 0)),
        out_shape=like(4, 2, SEND, width),
        compiler_params=pltpu.CompilerParams(vmem_limit_bytes=SCRATCH),
    )(ids, tokens, cotangent)
    part = exchange(own, "zl")
    part = small(widen_kernel, like(4, 2, 16, width), part, after=mates[:1])
    block, mates[1] = lax.optimization_barrier((exchange(part, AXES, first), mates[1]))
    other = from_other(block)
    part = experts(other, held + mates, experts(block, held + mates))
    total = jax.ShapeDtypeStruct((2, 16, width), jnp.float32)
    own, other = small(light_kernel, [total, like(2, 16, width)], exchange(part, AXES, first))
    part = small(pair_kernel, like(4, 2, SEND, width), own, from_other(other))
    part = exchange(part, "zl")
    mine = small(last_kernel, like(2, SEND, width), part)
    every = lax.all_gather(mine, ("zh", "c"), axis=0)
    return tuple(small(back_kernel, [like(count, width)] * 2, ids, every))


def solution(mesh):
    fine = Mesh(mesh.devices.reshape(SIZES), AXES)
    tensor, expert = ("y", "zl", "x"), ("zh", "c")
    placed = (
        P(tensor, None),
        P(tensor, None),
        P(tensor),
        P(expert, None, tensor),
        P(expert, None, tensor),
        P(expert, tensor, None),
    )
    return jax.shard_map(
        shards,
        mesh=fine,
        in_specs=placed,
        out_specs=(P(tensor, None), P(tensor, None)),
        check_vma=False,
    )
```

```python
import functools

import jax
import jax.numpy as jnp
from jax import lax
from jax.experimental import pallas as pl
from jax.experimental.pallas import tpu as pltpu
from jax.sharding import Mesh, PartitionSpec as P

SEND = 4
AXES = ("zh", "c", "y", "zl", "x")
SIZES = (4, 2, 4, 4, 4)
SCRATCH = 4 << 20
INSIDE = pl.BlockSpec(memory_space=pltpu.VMEM)


def device(zh, c, y, zl, x):
    return (((zh * 2 + c) * 4 + y) * 4 + zl) * 4 + x


def mixed_groups(first):
    groups = []
    for zh in range(4):
        for c in range(2):
            for zl in range(4):
                for still in range(4):
                    if (c == 0) == (first == "x"):
                        groups.append([device(zh, c, still, zl, k) for k in range(4)])
                    else:
                        groups.append([device(zh, c, k, zl, still) for k in range(4)])
    return groups


def ring_pairs(partner):
    pairs = []
    for zh in range(4):
        for zl in range(4):
            for p in range(4):
                for still in range(4):
                    q = partner(p)
                    pairs.append((device(zh, 0, p, zl, still), device(zh, 0, q, zl, still)))
                    pairs.append((device(zh, 1, still, zl, p), device(zh, 1, still, zl, q)))
    return pairs


def from_mate(array):
    return lax.ppermute(array, AXES, ring_pairs(lambda p: p ^ 1))


def from_other(array):
    return lax.ppermute(array, AXES, ring_pairs(lambda p: 3 - p))


def block_kernel(rows_ref, *refs):
    weights, beside, out_ref = refs[:6], refs[6:-1], refs[-1]
    for ref in beside:
        out_ref[:, 0] = ref[...]
        out_ref = out_ref.at[:, 1]
    gates, ups, downs = weights[0::3], weights[1::3], weights[2::3]
    width, hidden = gates[0].shape
    chunk = 1024
    deep = rows_ref.shape[0] * 16
    pieces = range(0, width, chunk)
    gates_of, ups_of, dhids_of = [], [], []
    for wg_ref, wu_ref, wd_ref in zip(gates, ups, downs):
        gu = dh = None
        for k in pieces:
            tok = rows_ref[:, 0, :, k : k + chunk].reshape(deep, chunk)
            cot = rows_ref[:, 1, :, k : k + chunk].reshape(deep, chunk)
            both = jnp.concatenate([wg_ref[k : k + chunk, :], wu_ref[k : k + chunk, :]], axis=1)
            one = jnp.dot(tok, both, preferred_element_type=jnp.float32)
            two = lax.dot_general(
                cot,
                wd_ref[:, k : k + chunk],
                (((1,), (1,)), ((), ())),
                preferred_element_type=jnp.float32,
            )
            gu, dh = (one, two) if gu is None else (gu + one, dh + two)
        gates_of.append(gu[:, :hidden])
        ups_of.append(gu[:, hidden:])
        dhids_of.append(dh)
    gate = jnp.concatenate(gates_of, axis=1)
    upper = jnp.concatenate(ups_of, axis=1)
    dhid = jnp.concatenate(dhids_of, axis=1)
    s = jax.nn.sigmoid(gate)
    hid = (gate * s * upper).astype(jnp.bfloat16)
    dgate = (dhid * upper * s * (1.0 + gate * (1.0 - s))).astype(jnp.bfloat16)
    dup = (dhid * gate * s).astype(jnp.bfloat16)
    for k in pieces:
        cut = slice(k, k + chunk)
        down = jnp.concatenate([ref[:, cut] for ref in downs])
        out = jnp.dot(hid, down, preferred_element_type=jnp.float32)
        out_ref[:, 0, :, cut] = out.astype(jnp.bfloat16).reshape(-1, 16, chunk)
        din = None
        for rows, refs_of in ((dgate, gates), (dup, ups)):
            both = jnp.concatenate([ref[cut, :] for ref in refs_of], axis=1)
            one = lax.dot_general(
                rows, both, (((1,), (1,)), ((), ())), preferred_element_type=jnp.float32
            )
            din = one if din is None else din + one
        out_ref[:, 1, :, cut] = din.astype(jnp.bfloat16).reshape(-1, 16, chunk)


def experts(block, weights, *beside):
    width, hidden = weights[0].shape
    count = block.shape[0] * 16
    return pl.pallas_call(
        block_kernel,
        in_specs=[INSIDE] * (7 + len(beside)),
        out_specs=INSIDE,
        out_shape=like(4, *[2] * len(beside), *block.shape[1:]),
        compiler_params=pltpu.CompilerParams(vmem_limit_bytes=24 << 20),
        cost_estimate=pl.CostEstimate(
            flops=24 * count * width * hidden,
            bytes_accessed=(6 << 20) + 8 * count * width,
            transcendentals=2 * count * hidden,
        ),
    )(block, *weights, *beside)


def widen_kernel(got_ref, out_ref):
    for i in range(2):
        rows = jnp.concatenate([got_ref[z, i].astype(jnp.float32) for z in range(4)])
        rows = rows.astype(jnp.bfloat16)
        for k in range(4):
            out_ref[k, i] = rows


def light_kernel(got_ref, own_ref, other_ref):
    for i, out_ref in enumerate((own_ref, other_ref)):
        total = got_ref[0, i].astype(jnp.float32)
        for k in range(1, 4):
            total += got_ref[k, i].astype(jnp.float32)
        out_ref[...] = total.astype(out_ref.dtype)


def pair_kernel(own_ref, got_ref, out_ref):
    for i in range(2):
        total = own_ref[i].astype(jnp.float32) + got_ref[i].astype(jnp.float32)
        for z in range(4):
            out_ref[z, i] = total[4 * z : 4 * z + 4].astype(jnp.bfloat16)


def last_kernel(got_ref, out_ref):
    for i in range(2):
        total = got_ref[0, i].astype(jnp.float32)
        for k in range(1, 4):
            total += got_ref[k, i].astype(jnp.float32)
        out_ref[i] = total.astype(jnp.bfloat16)


def columns_of(row):
    count = row.shape[1]
    at = lax.broadcasted_iota(jnp.int32, (count, count), 0)
    to = lax.broadcasted_iota(jnp.int32, (count, count), 1)
    return jnp.sum(jnp.where(at == to, row, 0), axis=1, keepdims=True)


def pick_kernel(id_ref, tokens_ref, grads_ref, out_ref):
    expert = lax.axis_index("zh") * 2 + lax.axis_index("c")
    row = id_ref[...]
    count = row.shape[1]
    at = lax.broadcasted_iota(jnp.int32, (count, count), 0)
    to = lax.broadcasted_iota(jnp.int32, (count, count), 1)
    same = (columns_of(row) == row) & (at < to)
    slot = jnp.sum(same.astype(jnp.int32), axis=0, keepdims=True)
    place = jnp.where(row == expert, slot, -1)
    wanted = lax.broadcasted_iota(jnp.int32, (8, count), 0)
    table = (wanted == place).astype(jnp.float32).astype(jnp.bfloat16)
    for i, ref in enumerate((tokens_ref, grads_ref)):
        rows = jnp.dot(table, ref[...], preferred_element_type=jnp.float32)
        for k in range(4):
            out_ref[k, i] = rows[:SEND].astype(jnp.bfloat16)


def back_kernel(id_ref, got_ref, *outs):
    row = id_ref[...]
    count = row.shape[1]
    column = columns_of(row)
    at = lax.broadcasted_iota(jnp.int32, (count, count), 0)
    to = lax.broadcasted_iota(jnp.int32, (count, count), 1)
    same = (column == row) & (to < at)
    slot = jnp.sum(same.astype(jnp.int32), axis=1, keepdims=True)
    cells = got_ref.shape[0] * SEND
    place = column * SEND + slot
    table = lax.broadcasted_iota(jnp.int32, (count, cells), 1) == place
    table = table.astype(jnp.float32).astype(jnp.bfloat16)
    for i, out in enumerate(outs):
        rows = jnp.concatenate([got_ref[e, i].astype(jnp.float32) for e in range(got_ref.shape[0])])
        out[...] = jnp.dot(
            table, rows.astype(jnp.bfloat16), preferred_element_type=jnp.float32
        ).astype(jnp.bfloat16)


def small(kernel, shapes, *arrays, after=()):
    size = sum(array.size for array in arrays)
    return pl.pallas_call(
        kernel,
        in_specs=[INSIDE] * len(arrays) + [pl.BlockSpec(memory_space=pl.ANY)] * len(after),
        out_specs=jax.tree.map(lambda _: INSIDE, shapes),
        out_shape=shapes,
        compiler_params=pltpu.CompilerParams(vmem_limit_bytes=SCRATCH),
        cost_estimate=pl.CostEstimate(flops=size, bytes_accessed=3 * size, transcendentals=0),
    )(*arrays, *after)


def like(*shape):
    return jax.ShapeDtypeStruct(shape, jnp.bfloat16)


def shards(tokens, cotangent, expert_id, gate_weight, up_weight, down_weight):
    count, width = tokens.shape
    ids = expert_id.reshape(1, count)
    first = mixed_groups("x")
    held = [gate_weight[0], up_weight[0], down_weight[0]]
    mates = [from_mate(weight) for weight in held]

    def exchange(blocks, axis, groups=None):
        return lax.all_to_all(blocks, axis, 0, 0, axis_index_groups=groups, tiled=True)

    own = pl.pallas_call(
        pick_kernel,
        grid=(1,),
        in_specs=[
            pl.BlockSpec((1, count), lambda i: (0, 0)),
            pl.BlockSpec((count, width), lambda i: (0, 0)),
            pl.BlockSpec((count, width), lambda i: (0, 0)),
        ],
        out_specs=pl.BlockSpec((4, 2, SEND, width), lambda i: (0, 0, 0, 0)),
        out_shape=like(4, 2, SEND, width),
        compiler_params=pltpu.CompilerParams(vmem_limit_bytes=SCRATCH),
    )(ids, tokens, cotangent)
    part = exchange(own, "zl")
    part = small(widen_kernel, like(4, 2, 16, width), part)
    block, mates[0], mates[1] = lax.optimization_barrier(
        (exchange(part, AXES, first), mates[0], mates[1])
    )
    other = from_other(block)
    part = experts(other, held + mates, experts(block, held + mates))
    total = jax.ShapeDtypeStruct((2, 16, width), jnp.float32)
    own, other = small(light_kernel, [total, like(2, 16, width)], exchange(part, AXES, first))
    part = small(pair_kernel, like(4, 2, SEND, width), own, from_other(other))
    part = exchange(part, "zl")
    mine = small(last_kernel, like(2, SEND, width), part)
    every = lax.all_gather(mine, ("zh", "c"), axis=0)
    return tuple(small(back_kernel, [like(count, width)] * 2, ids, every))


def solution(mesh):
    fine = Mesh(mesh.devices.reshape(SIZES), AXES)
    tensor, expert = ("y", "zl", "x"), ("zh", "c")
    placed = (
        P(tensor, None),
        P(tensor, None),
        P(tensor),
        P(expert, None, tensor),
        P(expert, None, tensor),
        P(expert, tensor, None),
    )
    return jax.shard_map(
        shards,
        mesh=fine,
        in_specs=placed,
        out_specs=(P(tensor, None), P(tensor, None)),
        check_vma=False,
    )
```

```python
import functools

import jax
import jax.numpy as jnp
from jax import lax
from jax.experimental import pallas as pl
from jax.experimental.pallas import tpu as pltpu
from jax.sharding import Mesh, PartitionSpec as P

SEND = 4
AXES = ("zh", "c", "y", "zl", "x")
SIZES = (4, 2, 4, 4, 4)
SCRATCH = 4 << 20
INSIDE = pl.BlockSpec(memory_space=pltpu.VMEM)


def device(zh, c, y, zl, x):
    return (((zh * 2 + c) * 4 + y) * 4 + zl) * 4 + x


def mixed_groups(first):
    groups = []
    for zh in range(4):
        for c in range(2):
            for zl in range(4):
                for still in range(4):
                    if (c == 0) == (first == "x"):
                        groups.append([device(zh, c, still, zl, k) for k in range(4)])
                    else:
                        groups.append([device(zh, c, k, zl, still) for k in range(4)])
    return groups


def ring_pairs(partner):
    pairs = []
    for zh in range(4):
        for zl in range(4):
            for p in range(4):
                for still in range(4):
                    q = partner(p)
                    pairs.append((device(zh, 0, p, zl, still), device(zh, 0, q, zl, still)))
                    pairs.append((device(zh, 1, still, zl, p), device(zh, 1, still, zl, q)))
    return pairs


def from_mate(array):
    return lax.ppermute(array, AXES, ring_pairs(lambda p: p ^ 1))


def from_other(array):
    return lax.ppermute(array, AXES, ring_pairs(lambda p: 3 - p))


def block_kernel(fetch, rows_ref, *refs):
    copies = []
    if fetch:
        given, out_ref, weights, sems = refs[:6], refs[6], refs[7:13], refs[13]
        for i, (one, two) in enumerate(zip(given, weights)):
            copies.append(pltpu.make_async_copy(one, two, sems.at[i]))
            copies[i].start()
    else:
        weights, beside_ref, out_ref = refs[:6], refs[6], refs[7]
        out_ref[:, 0] = beside_ref[...]
        out_ref = out_ref.at[:, 1]
    gates, ups, downs = weights[0::3], weights[1::3], weights[2::3]
    width, hidden = gates[0].shape
    chunk = 1024
    deep = rows_ref.shape[0] * 16
    pieces = range(0, width, chunk)
    gates_of, ups_of, dhids_of = [], [], []
    for i, (wg_ref, wu_ref, wd_ref) in enumerate(zip(gates, ups, downs)):
        for copy in copies[3 * i : 3 * i + 3]:
            copy.wait()
        gu = dh = None
        for k in pieces:
            tok = rows_ref[:, 0, :, k : k + chunk].reshape(deep, chunk)
            cot = rows_ref[:, 1, :, k : k + chunk].reshape(deep, chunk)
            both = jnp.concatenate([wg_ref[k : k + chunk, :], wu_ref[k : k + chunk, :]], axis=1)
            one = jnp.dot(tok, both, preferred_element_type=jnp.float32)
            two = lax.dot_general(
                cot,
                wd_ref[:, k : k + chunk],
                (((1,), (1,)), ((), ())),
                preferred_element_type=jnp.float32,
            )
            gu, dh = (one, two) if gu is None else (gu + one, dh + two)
        gates_of.append(gu[:, :hidden])
        ups_of.append(gu[:, hidden:])
        dhids_of.append(dh)
    gate = jnp.concatenate(gates_of, axis=1)
    upper = jnp.concatenate(ups_of, axis=1)
    dhid = jnp.concatenate(dhids_of, axis=1)
    s = jax.nn.sigmoid(gate)
    hid = (gate * s * upper).astype(jnp.bfloat16)
    dgate = (dhid * upper * s * (1.0 + gate * (1.0 - s))).astype(jnp.bfloat16)
    dup = (dhid * gate * s).astype(jnp.bfloat16)
    for k in pieces:
        cut = slice(k, k + chunk)
        down = jnp.concatenate([ref[:, cut] for ref in downs])
        out = jnp.dot(hid, down, preferred_element_type=jnp.float32)
        out_ref[:, 0, :, cut] = out.astype(jnp.bfloat16).reshape(-1, 16, chunk)
        din = None
        for rows, refs_of in ((dgate, gates), (dup, ups)):
            both = jnp.concatenate([ref[cut, :] for ref in refs_of], axis=1)
            one = lax.dot_general(
                rows, both, (((1,), (1,)), ((), ())), preferred_element_type=jnp.float32
            )
            din = one if din is None else din + one
        out_ref[:, 1, :, cut] = din.astype(jnp.bfloat16).reshape(-1, 16, chunk)


def experts(block, weights, beside=None):
    width, hidden = weights[0].shape
    count = block.shape[0] * 16
    cost = pl.CostEstimate(
        flops=24 * count * width * hidden,
        bytes_accessed=(6 << 20) + 8 * count * width,
        transcendentals=2 * count * hidden,
    )
    params = pltpu.CompilerParams(vmem_limit_bytes=24 << 20)
    if beside is None:
        return pl.pallas_call(
            functools.partial(block_kernel, True),
            in_specs=[INSIDE] + [pl.BlockSpec(memory_space=pl.ANY)] * 6,
            out_specs=[INSIDE] * 7,
            out_shape=[like(*block.shape)] + [like(*weight.shape) for weight in weights],
            scratch_shapes=[pltpu.SemaphoreType.DMA((6,))],
            compiler_params=params,
            cost_estimate=cost,
        )(block, *weights)
    return pl.pallas_call(
        functools.partial(block_kernel, False),
        in_specs=[INSIDE] * 8,
        out_specs=INSIDE,
        out_shape=like(4, 2, *block.shape[1:]),
        compiler_params=params,
        cost_estimate=cost,
    )(block, *weights, beside)


def widen_kernel(got_ref, _, out_ref):
    for i in range(2):
        rows = jnp.concatenate([got_ref[z, i].astype(jnp.float32) for z in range(4)])
        rows = rows.astype(jnp.bfloat16)
        for k in range(4):
            out_ref[k, i] = rows


def light_kernel(got_ref, own_ref, other_ref):
    for i, out_ref in enumerate((own_ref, other_ref)):
        total = got_ref[0, i].astype(jnp.float32)
        for k in range(1, 4):
            total += got_ref[k, i].astype(jnp.float32)
        out_ref[...] = total.astype(out_ref.dtype)


def pair_kernel(own_ref, got_ref, out_ref):
    for i in range(2):
        total = own_ref[i].astype(jnp.float32) + got_ref[i].astype(jnp.float32)
        for z in range(4):
            out_ref[z, i] = total[4 * z : 4 * z + 4].astype(jnp.bfloat16)


def last_kernel(got_ref, out_ref):
    for i in range(2):
        total = got_ref[0, i].astype(jnp.float32)
        for k in range(1, 4):
            total += got_ref[k, i].astype(jnp.float32)
        out_ref[i] = total.astype(jnp.bfloat16)


def columns_of(row):
    count = row.shape[1]
    at = lax.broadcasted_iota(jnp.int32, (count, count), 0)
    to = lax.broadcasted_iota(jnp.int32, (count, count), 1)
    return jnp.sum(jnp.where(at == to, row, 0), axis=1, keepdims=True)


def pick_kernel(id_ref, tokens_ref, grads_ref, out_ref):
    expert = lax.axis_index("zh") * 2 + lax.axis_index("c")
    row = id_ref[...]
    count = row.shape[1]
    at = lax.broadcasted_iota(jnp.int32, (count, count), 0)
    to = lax.broadcasted_iota(jnp.int32, (count, count), 1)
    same = (columns_of(row) == row) & (at < to)
    slot = jnp.sum(same.astype(jnp.int32), axis=0, keepdims=True)
    place = jnp.where(row == expert, slot, -1)
    wanted = lax.broadcasted_iota(jnp.int32, (8, count), 0)
    table = (wanted == place).astype(jnp.float32).astype(jnp.bfloat16)
    for i, ref in enumerate((tokens_ref, grads_ref)):
        rows = jnp.dot(table, ref[...], preferred_element_type=jnp.float32)
        for k in range(4):
            out_ref[k, i] = rows[:SEND].astype(jnp.bfloat16)


def back_kernel(id_ref, got_ref, *outs):
    row = id_ref[...]
    count = row.shape[1]
    column = columns_of(row)
    at = lax.broadcasted_iota(jnp.int32, (count, count), 0)
    to = lax.broadcasted_iota(jnp.int32, (count, count), 1)
    same = (column == row) & (to < at)
    slot = jnp.sum(same.astype(jnp.int32), axis=1, keepdims=True)
    cells = got_ref.shape[0] * SEND
    place = column * SEND + slot
    table = lax.broadcasted_iota(jnp.int32, (count, cells), 1) == place
    table = table.astype(jnp.float32).astype(jnp.bfloat16)
    for i, out in enumerate(outs):
        rows = jnp.concatenate([got_ref[e, i].astype(jnp.float32) for e in range(got_ref.shape[0])])
        out[...] = jnp.dot(
            table, rows.astype(jnp.bfloat16), preferred_element_type=jnp.float32
        ).astype(jnp.bfloat16)


def small(kernel, shapes, *arrays, after=()):
    size = sum(array.size for array in arrays)
    return pl.pallas_call(
        kernel,
        in_specs=[INSIDE] * len(arrays) + [pl.BlockSpec(memory_space=pl.ANY)] * len(after),
        out_specs=jax.tree.map(lambda _: INSIDE, shapes),
        out_shape=shapes,
        compiler_params=pltpu.CompilerParams(vmem_limit_bytes=SCRATCH),
        cost_estimate=pl.CostEstimate(flops=size, bytes_accessed=3 * size, transcendentals=0),
    )(*arrays, *after)


def like(*shape):
    return jax.ShapeDtypeStruct(shape, jnp.bfloat16)


def shards(tokens, cotangent, expert_id, gate_weight, up_weight, down_weight):
    count, width = tokens.shape
    ids = expert_id.reshape(1, count)
    first = mixed_groups("x")
    held = [gate_weight[0], up_weight[0], down_weight[0]]
    mates = [from_mate(weight) for weight in held]

    def exchange(blocks, axis, groups=None):
        return lax.all_to_all(blocks, axis, 0, 0, axis_index_groups=groups, tiled=True)

    own = pl.pallas_call(
        pick_kernel,
        grid=(1,),
        in_specs=[
            pl.BlockSpec((1, count), lambda i: (0, 0)),
            pl.BlockSpec((count, width), lambda i: (0, 0)),
            pl.BlockSpec((count, width), lambda i: (0, 0)),
        ],
        out_specs=pl.BlockSpec((4, 2, SEND, width), lambda i: (0, 0, 0, 0)),
        out_shape=like(4, 2, SEND, width),
        compiler_params=pltpu.CompilerParams(vmem_limit_bytes=SCRATCH),
    )(ids, tokens, cotangent)
    part = exchange(own, "zl")
    part = small(widen_kernel, like(4, 2, 16, width), part, after=mates[:1])
    block, mates[1] = lax.optimization_barrier((exchange(part, AXES, first), mates[1]))
    other = from_other(block)
    own, *weights = experts(block, held + mates)
    part = experts(other, weights, own)
    total = jax.ShapeDtypeStruct((2, 16, width), jnp.float32)
    own, other = small(light_kernel, [total, like(2, 16, width)], exchange(part, AXES, first))
    part = small(pair_kernel, like(4, 2, SEND, width), own, from_other(other))
    part = exchange(part, "zl")
    mine = small(last_kernel, like(2, SEND, width), part)
    every = lax.all_gather(mine, ("zh", "c"), axis=0)
    return tuple(small(back_kernel, [like(count, width)] * 2, ids, every))


def solution(mesh):
    fine = Mesh(mesh.devices.reshape(SIZES), AXES)
    tensor, expert = ("y", "zl", "x"), ("zh", "c")
    placed = (
        P(tensor, None),
        P(tensor, None),
        P(tensor),
        P(expert, None, tensor),
        P(expert, None, tensor),
        P(expert, tensor, None),
    )
    return jax.shard_map(
        shards,
        mesh=fine,
        in_specs=placed,
        out_specs=(P(tensor, None), P(tensor, None)),
        check_vma=False,
    )
```

```python
import functools

import jax
import jax.numpy as jnp
from jax import lax
from jax.experimental import pallas as pl
from jax.experimental.pallas import tpu as pltpu
from jax.sharding import Mesh, PartitionSpec as P

SEND = 4
AXES = ("zh", "c", "y", "zl", "x")
SIZES = (4, 2, 4, 4, 4)
SCRATCH = 4 << 20
INSIDE = pl.BlockSpec(memory_space=pltpu.VMEM)


def device(zh, c, y, zl, x):
    return (((zh * 2 + c) * 4 + y) * 4 + zl) * 4 + x


def mixed_groups(first):
    groups = []
    for zh in range(4):
        for c in range(2):
            for zl in range(4):
                for still in range(4):
                    if (c == 0) == (first == "x"):
                        groups.append([device(zh, c, still, zl, k) for k in range(4)])
                    else:
                        groups.append([device(zh, c, k, zl, still) for k in range(4)])
    return groups


def ring_pairs(partner):
    pairs = []
    for zh in range(4):
        for zl in range(4):
            for p in range(4):
                for still in range(4):
                    q = partner(p)
                    pairs.append((device(zh, 0, p, zl, still), device(zh, 0, q, zl, still)))
                    pairs.append((device(zh, 1, still, zl, p), device(zh, 1, still, zl, q)))
    return pairs


def from_mate(array):
    return lax.ppermute(array, AXES, ring_pairs(lambda p: p ^ 1))


def from_other(array):
    return lax.ppermute(array, AXES, ring_pairs(lambda p: 3 - p))


def block_kernel(fetch, rows_ref, *refs):
    copies = []
    if fetch:
        given, out_ref, weights, sems = refs[:6], refs[6], refs[7:13], refs[13]
        for i, (one, two) in enumerate(zip(given, weights)):
            copies.append(pltpu.make_async_copy(one, two, sems.at[i]))
            copies[i].start()
    else:
        weights, beside_ref, out_ref = refs[:6], refs[6], refs[7]
        out_ref[:, 0] = beside_ref[...]
        out_ref = out_ref.at[:, 1]
    gates, ups, downs = weights[0::3], weights[1::3], weights[2::3]
    width, hidden = gates[0].shape
    chunk = 1024
    deep = rows_ref.shape[0] * 16
    pieces = range(0, width, chunk)
    gates_of, ups_of, dhids_of = [], [], []
    for i, (wg_ref, wu_ref, wd_ref) in enumerate(zip(gates, ups, downs)):
        for copy in copies[3 * i : 3 * i + 3]:
            copy.wait()
        gu = dh = None
        for k in pieces:
            tok = rows_ref[:, 0, :, k : k + chunk].reshape(deep, chunk)
            cot = rows_ref[:, 1, :, k : k + chunk].reshape(deep, chunk)
            both = jnp.concatenate([wg_ref[k : k + chunk, :], wu_ref[k : k + chunk, :]], axis=1)
            one = jnp.dot(tok, both, preferred_element_type=jnp.float32)
            two = lax.dot_general(
                cot,
                wd_ref[:, k : k + chunk],
                (((1,), (1,)), ((), ())),
                preferred_element_type=jnp.float32,
            )
            gu, dh = (one, two) if gu is None else (gu + one, dh + two)
        gates_of.append(gu[:, :hidden])
        ups_of.append(gu[:, hidden:])
        dhids_of.append(dh)
    gate = jnp.concatenate(gates_of, axis=1)
    upper = jnp.concatenate(ups_of, axis=1)
    dhid = jnp.concatenate(dhids_of, axis=1)
    s = jax.nn.sigmoid(gate)
    hid = (gate * s * upper).astype(jnp.bfloat16)
    dgate = (dhid * upper * s * (1.0 + gate * (1.0 - s))).astype(jnp.bfloat16)
    dup = (dhid * gate * s).astype(jnp.bfloat16)
    for k in pieces:
        cut = slice(k, k + chunk)
        down = jnp.concatenate([ref[:, cut] for ref in downs])
        out = jnp.dot(hid, down, preferred_element_type=jnp.float32)
        out_ref[:, 0, :, cut] = out.astype(jnp.bfloat16).reshape(-1, 16, chunk)
        din = None
        for rows, refs_of in ((dgate, gates), (dup, ups)):
            both = jnp.concatenate([ref[cut, :] for ref in refs_of], axis=1)
            one = lax.dot_general(
                rows, both, (((1,), (1,)), ((), ())), preferred_element_type=jnp.float32
            )
            din = one if din is None else din + one
        out_ref[:, 1, :, cut] = din.astype(jnp.bfloat16).reshape(-1, 16, chunk)


def experts(block, weights, beside=None):
    width, hidden = weights[0].shape
    count = block.shape[0] * 16
    cost = pl.CostEstimate(
        flops=24 * count * width * hidden,
        bytes_accessed=(6 << 20) + 8 * count * width,
        transcendentals=2 * count * hidden,
    )
    params = pltpu.CompilerParams(vmem_limit_bytes=24 << 20)
    if beside is None:
        return pl.pallas_call(
            functools.partial(block_kernel, True),
            in_specs=[INSIDE] + [pl.BlockSpec(memory_space=pl.ANY)] * 6,
            out_specs=[INSIDE] * 7,
            out_shape=[like(*block.shape)] + [like(*weight.shape) for weight in weights],
            scratch_shapes=[pltpu.SemaphoreType.DMA((6,))],
            compiler_params=params,
            cost_estimate=cost,
        )(block, *weights)
    return pl.pallas_call(
        functools.partial(block_kernel, False),
        in_specs=[INSIDE] * 8,
        out_specs=INSIDE,
        out_shape=like(4, 2, *block.shape[1:]),
        compiler_params=params,
        cost_estimate=cost,
    )(block, *weights, beside)


def widen_kernel(got_ref, _, out_ref):
    for i in range(2):
        rows = jnp.concatenate([got_ref[z, i].astype(jnp.float32) for z in range(4)])
        rows = rows.astype(jnp.bfloat16)
        for k in range(4):
            out_ref[k, i] = rows


def light_kernel(got_ref, own_ref, other_ref):
    for i, out_ref in enumerate((own_ref, other_ref)):
        total = got_ref[0, i].astype(jnp.float32)
        for k in range(1, 4):
            total += got_ref[k, i].astype(jnp.float32)
        out_ref[...] = total.astype(out_ref.dtype)


def pair_kernel(own_ref, got_ref, out_ref):
    for i in range(2):
        total = own_ref[i].astype(jnp.float32) + got_ref[i].astype(jnp.float32)
        for z in range(4):
            out_ref[z, i] = total[4 * z : 4 * z + 4].astype(jnp.bfloat16)


def last_kernel(got_ref, out_ref):
    for i in range(2):
        total = got_ref[0, i].astype(jnp.float32)
        for k in range(1, 4):
            total += got_ref[k, i].astype(jnp.float32)
        out_ref[i] = total.astype(jnp.bfloat16)


def columns_of(row):
    count = row.shape[1]
    at = lax.broadcasted_iota(jnp.int32, (count, count), 0)
    to = lax.broadcasted_iota(jnp.int32, (count, count), 1)
    return jnp.sum(jnp.where(at == to, row, 0), axis=1, keepdims=True)


def pick_kernel(id_ref, tokens_ref, grads_ref, out_ref):
    expert = lax.axis_index("zh") * 2 + lax.axis_index("c")
    row = id_ref[...]
    count = row.shape[1]
    at = lax.broadcasted_iota(jnp.int32, (count, count), 0)
    to = lax.broadcasted_iota(jnp.int32, (count, count), 1)
    same = (columns_of(row) == row) & (at < to)
    slot = jnp.sum(same.astype(jnp.int32), axis=0, keepdims=True)
    place = jnp.where(row == expert, slot, -1)
    wanted = lax.broadcasted_iota(jnp.int32, (8, count), 0)
    table = (wanted == place).astype(jnp.float32).astype(jnp.bfloat16)
    for i, ref in enumerate((tokens_ref, grads_ref)):
        rows = jnp.dot(table, ref[...], preferred_element_type=jnp.float32)
        for k in range(4):
            out_ref[k, i] = rows[:SEND].astype(jnp.bfloat16)


def back_kernel(id_ref, got_ref, *outs):
    row = id_ref[...]
    count = row.shape[1]
    column = columns_of(row)
    at = lax.broadcasted_iota(jnp.int32, (count, count), 0)
    to = lax.broadcasted_iota(jnp.int32, (count, count), 1)
    same = (column == row) & (to < at)
    slot = jnp.sum(same.astype(jnp.int32), axis=1, keepdims=True)
    cells = got_ref.shape[0] * SEND
    place = column * SEND + slot
    table = lax.broadcasted_iota(jnp.int32, (count, cells), 1) == place
    table = table.astype(jnp.float32).astype(jnp.bfloat16)
    for i, out in enumerate(outs):
        rows = jnp.concatenate([got_ref[e, i].astype(jnp.float32) for e in range(got_ref.shape[0])])
        out[...] = jnp.dot(
            table, rows.astype(jnp.bfloat16), preferred_element_type=jnp.float32
        ).astype(jnp.bfloat16)


def small(kernel, shapes, *arrays, after=()):
    size = sum(array.size for array in arrays)
    return pl.pallas_call(
        kernel,
        in_specs=[INSIDE] * len(arrays) + [pl.BlockSpec(memory_space=pl.ANY)] * len(after),
        out_specs=jax.tree.map(lambda _: INSIDE, shapes),
        out_shape=shapes,
        compiler_params=pltpu.CompilerParams(vmem_limit_bytes=SCRATCH),
        cost_estimate=pl.CostEstimate(flops=size, bytes_accessed=3 * size, transcendentals=0),
    )(*arrays, *after)


def like(*shape):
    return jax.ShapeDtypeStruct(shape, jnp.bfloat16)


def shards(tokens, cotangent, expert_id, gate_weight, up_weight, down_weight):
    count, width = tokens.shape
    ids = expert_id.reshape(1, count)
    first = mixed_groups("x")
    held = [gate_weight[0], up_weight[0], down_weight[0]]
    mates = [from_mate(weight) for weight in held[:2]]
    mates[1], down = lax.optimization_barrier((mates[1], held[2]))
    mates.append(from_mate(down))

    def exchange(blocks, axis, groups=None):
        return lax.all_to_all(blocks, axis, 0, 0, axis_index_groups=groups, tiled=True)

    own = pl.pallas_call(
        pick_kernel,
        grid=(1,),
        in_specs=[
            pl.BlockSpec((1, count), lambda i: (0, 0)),
            pl.BlockSpec((count, width), lambda i: (0, 0)),
            pl.BlockSpec((count, width), lambda i: (0, 0)),
        ],
        out_specs=pl.BlockSpec((4, 2, SEND, width), lambda i: (0, 0, 0, 0)),
        out_shape=like(4, 2, SEND, width),
        compiler_params=pltpu.CompilerParams(vmem_limit_bytes=SCRATCH),
    )(ids, tokens, cotangent)
    part = exchange(own, "zl")
    part = small(widen_kernel, like(4, 2, 16, width), part, after=mates[:1])
    block, mates[1] = lax.optimization_barrier((exchange(part, AXES, first), mates[1]))
    other = from_other(block)
    own, *weights = experts(block, held + mates)
    part = experts(other, weights, own)
    total = jax.ShapeDtypeStruct((2, 16, width), jnp.float32)
    own, other = small(light_kernel, [total, like(2, 16, width)], exchange(part, AXES, first))
    part = small(pair_kernel, like(4, 2, SEND, width), own, from_other(other))
    part = exchange(part, "zl")
    mine = small(last_kernel, like(2, SEND, width), part)
    every = lax.all_gather(mine, ("zh", "c"), axis=0)
    return tuple(small(back_kernel, [like(count, width)] * 2, ids, every))


def solution(mesh):
    fine = Mesh(mesh.devices.reshape(SIZES), AXES)
    tensor, expert = ("y", "zl", "x"), ("zh", "c")
    placed = (
        P(tensor, None),
        P(tensor, None),
        P(tensor),
        P(expert, None, tensor),
        P(expert, None, tensor),
        P(expert, tensor, None),
    )
    return jax.shard_map(
        shards,
        mesh=fine,
        in_specs=placed,
        out_specs=(P(tensor, None), P(tensor, None)),
        check_vma=False,
    )
```
